256 devices in a mesh: dp: 64 (over z, x, core), tensor: 4 (over y).
Axes of the slice: x: 4, y: 4, z: 8, core: 2. Of those that a mesh axis runs over, the one named last changes fastest.
Arguments:
- hidden_acts: bfloat16 [64, 768, 896], P('dp', None, 'tensor'), may hold values from -6 to 6
- out_grads: bfloat16 [768, 16384], P('dp', 'tensor'), may hold values from -0.21875 to 0.21875
- residual_in: bfloat16 [64, 896, 8192], P('dp', 'tensor'), may hold values from -6 to 6
- q_prev: bfloat16 [8192, 32], replicated, may hold values from -0.0625 to 0.0625
Outputs:
- p_basis: float32 [28672, 32], P('tensor')
- q_new: float32 [8192, 32], P('dp')
- residual_out: bfloat16 [64, 896, 8192], P('dp', 'tensor')
The draws below stay inside these ranges and needn't reach their ends.
All inputs are finite; a program needn't handle non-finite values.
Results may differ from the reference program's by a relative error of at most 0.0051.
Values may be sent and summed in bfloat16 or wider, within the bound.
A program may use at most 192 MiB of HBM per device.

```python
import jax
import jax.numpy as jnp
from jax import lax

D = 8192
ROWS = 28672
RANK = 32
REPLICAS = 2
TOK_DEV = 768
PIECES = 32
ROWS_DEV = 224
SLAB = 896
N_DP = 64
N_TENSOR = 4


def shard_levels(key, extent, shards, smallest, high):
    def one(axis_at, blocks):
        steps = jax.random.uniform(jax.random.fold_in(jax.random.fold_in(key, 6), axis_at), (blocks,), jnp.float32, smallest / len(shards), high / len(shards))
        return jnp.repeat(jnp.exp(steps), extent[axis_at] // blocks).reshape((-1,) + (1,) * (len(extent) - axis_at - 1))

    level = one(*shards[0])
    for cut in shards[1:]:
        level = level * one(*cut)
    return level


def scatter_about(own_key, extent, width, most, split=(), kind=jnp.bfloat16):
    result = width * jax.random.normal(own_key, extent, jnp.float32)
    if split:
        result = result * shard_levels(own_key, extent, split, -0.22, 0.18)
    return jnp.clip(result, -most, most).astype(kind)


def setup_inputs(seed: int = 0) -> dict:
    arg_keys = jax.random.split(jax.random.key(seed), 5)
    return {
        "hidden_acts": scatter_about(arg_keys[0], (N_DP, TOK_DEV, SLAB), 1.0, 6.0, ((0, 64), (2, 4))),
        "out_grads": scatter_about(arg_keys[1], (TOK_DEV, REPLICAS * D), TOK_DEV ** -0.5, 0.21875, ((0, 64), (1, 4))),
        "residual_in": scatter_about(arg_keys[2], (N_DP, SLAB, D), 1.0, 6.0, ((0, 64), (1, 4))),
        "q_prev": scatter_about(arg_keys[3], (D, RANK), D ** -0.5, 0.0625),
    }


def reference(hidden_acts, out_grads, residual_in, q_prev):
    hidden = hidden_acts.reshape(REPLICAS, PIECES, TOK_DEV, N_TENSOR, ROWS_DEV).transpose(0, 2, 3, 1, 4).reshape(REPLICAS, TOK_DEV, ROWS)
    out_blocks = out_grads.reshape(TOK_DEV, N_TENSOR, REPLICAS, D // N_TENSOR).transpose(2, 0, 1, 3).reshape(REPLICAS, TOK_DEV, D)
    resid = residual_in.reshape(REPLICAS, PIECES, N_TENSOR, ROWS_DEV, D).transpose(0, 2, 1, 3, 4).reshape(REPLICAS, ROWS, D)

    def replica_step(running, pieces_in):
        hidden_one, grads_one, resid_one = pieces_in
        gradient = jnp.dot(hidden_one.T.astype(jnp.float32), grads_one.astype(jnp.float32), preferred_element_type=jnp.float32)
        merged = (gradient + resid_one.astype(jnp.float32)).astype(jnp.bfloat16)
        running = running + jnp.dot(merged.astype(jnp.float32), q_prev.astype(jnp.float32), preferred_element_type=jnp.float32)
        return (running, merged)
    p_sum, merged = lax.scan(replica_step, jnp.zeros((ROWS, RANK), jnp.float32), (hidden, out_blocks, resid))
    gram_matrix = jnp.dot(p_sum.T.astype(jnp.float32), p_sum.astype(jnp.float32), precision=lax.Precision.HIGHEST, preferred_element_type=jnp.float32)
    factor = jnp.linalg.cholesky(gram_matrix)
    p_basis = lax.linalg.triangular_solve(factor, p_sum, left_side=False, lower=True, transpose_a=True)
    p_low = p_basis.astype(jnp.bfloat16)

    def q_step(running, merged_one):
        return (running + jnp.dot(merged_one.T.astype(jnp.float32), p_low.astype(jnp.float32), preferred_element_type=jnp.float32), None)
    q_sum, unused = lax.scan(q_step, jnp.zeros((D, RANK), jnp.float32), merged)
    q_new = q_sum / REPLICAS
    q_low = q_new.astype(jnp.bfloat16)
    approx = jnp.dot(p_low.astype(jnp.float32), q_low.T.astype(jnp.float32), preferred_element_type=jnp.float32)

    def new_residual(merged_one):
        return (merged_one.astype(jnp.float32) - approx).astype(jnp.bfloat16)
    residual_all = lax.map(new_residual, merged)
    residual_out = residual_all.reshape(REPLICAS, N_TENSOR, PIECES, ROWS_DEV, D).transpose(0, 2, 1, 3, 4).reshape(N_DP, SLAB, D)
    return (p_basis, q_new, residual_out)
```

```python
import jax
import jax.numpy as jnp
from jax import lax
from jax.experimental import pallas as pl
from jax.experimental.pallas import tpu as pltpu
from jax.sharding import PartitionSpec as P

NZ, NX, NC, NY = 8, 4, 2, 4
RANK = 32
TOK, TOK_DEV = 768, 12
ROWS = 224
D = 8192
PAD = 256
NQ = 4
DEEP = 2
F32, BF16 = jnp.float32, jnp.bfloat16
HIGH = lax.Precision.HIGHEST
MESH = pl.DeviceIdType.MESH


def link_of(h, axis, step):
    return 2 * ((axis + h) % 2) + (0 if step == 1 else 1)


def plan():
    hop, lat, core_lat, work = 2.1, 2.8, 1.6, 0.65
    now, count, order, arrivals = 0.0, 0, [], []
    parts, both = {}, {}
    queue, done, free = [[] for _ in range(4)], [[] for _ in range(4)], [0.0] * 4
    starts = [(4.6 + 2.1 * h, h) for h in range(NQ)]
    todo = [(h, rel) for h in range(NQ) for rel in (0, 3, 1, 2)]

    def put(kind, size, key, push):
        nonlocal count
        count += 1
        queue[link_of(push[0], push[4], push[5])].append(((kind, push[0], count), size, key, push))

    def spread(h, f):
        put(2, 1.0, (h, f, 3), (h, f, 0, None, 1, 1))
        put(2, 1.0, (h, f, 1), (h, f, 0, None, 1, -1))

    while len(order) < NQ * 40:
        arrivals.sort()
        if starts and starts[0][0] <= now:
            h = starts.pop(0)[1]
            order.append(("begin", h))
            now += 0.3
            put(0, 1.0, (h, 3, 0), (h, 0, 0, None, 0, 1))
            put(0, 1.0, (h, 1, 0), (h, 0, 0, None, 0, -1))
            spread(h, 0)
            both[h, 0, 0] = now + core_lat
            continue
        if arrivals and arrivals[0][0] <= now:
            h, f, s = arrivals.pop(0)[1]
            if f == 2 and s == 0 or s == 2:
                parts[h, f, s] = parts.get((h, f, s), 0) + 1
                if parts[h, f, s] < 2:
                    continue
            order.append(("forward", h, f, s))
            if s == 0:
                if f != 2:
                    step = 1 if f == 3 else -1
                    put(1, 0.5, (h, 2, 0), (h, f, 0, 0 if f == 3 else 1, 0, step))
                spread(h, f)
            elif s != 2:
                step = 1 if s == 3 else -1
                put(3, 0.5, (h, f, 2), (h, f, s, 0 if s == 3 else 1, 1, step))
            both[h, f, s] = now + core_lat
            now += 0.08
            continue
        sent = False
        for link in range(4):
            if queue[link] and (len(done[link]) < DEEP or done[link][-DEEP] <= now):
                queue[link].sort()
                _, size, key, push = queue[link].pop(0)
                free[link] = max(now, free[link]) + size * hop
                done[link].append(free[link])
                arrivals.append((free[link] + lat, key))
                order.append(("push",) + push)
                now += 0.04
                sent = True
                break
        if sent:
            continue
        ready = None
        for h, rel in todo:
            need = [(h, i, rel) if h % 2 == 0 else (h, rel, i) for i in range(4)]
            if all(both.get(k, 1e9) <= now for k in need):
                ready = (h, rel)
                break
        if ready:
            todo.remove(ready)
            order.append(("compute",) + ready)
            now += work
            continue
        times = [t for t, _ in arrivals[:1]] + [t for t, _ in starts[:1]]
        times += [t for t in both.values() if t > now]
        times += [
            done[link][-DEEP] for link in range(4)
            if queue[link] and len(done[link]) >= DEEP and done[link][-DEEP] > now
        ]
        now = max(now + 1e-3, min(times))
    return order


ORDER = plan()


def iota(shape, axis):
    return lax.broadcasted_iota(jnp.int32, shape, axis)


def div12(v):
    return (v * 5462) >> 16


def one_hot(cond):
    return jnp.where(cond, 1.0, 0.0).astype(BF16)


def dot(a, b, dims=((1,), (0,)), precision=None):
    return lax.dot_general(
        a, b, (dims, ((), ())), precision=precision, preferred_element_type=F32
    )


def eliminate(gram):
    row, lane = iota((RANK, 128), 0), iota((RANK, 128), 1)
    work = gram + jnp.where(lane == row + RANK, 1.0, 0.0)
    for k in range(RANK):
        column = jnp.broadcast_to(work[:, k:k + 1], (RANK, 128))
        scale = lax.rsqrt(column[k:k + 1, :])
        pivot_row = work[k:k + 1, :] * scale
        below = work - (column * scale) * pivot_row
        work = jnp.where(row > k, below, jnp.where(row == k, pivot_row, work))
    inverse = pltpu.roll(work, 128 - RANK, 1)
    return jnp.where(lane < RANK, inverse, 0.0)


def main_kernel(
    hid_hbm, og_hbm, q_hbm, res_hbm,
    mer_out, pb_out, qt_out, low_out,
    hid, og, pack, zbuf, grads, hid_t, res, mer, qv, pacc, pt_mine, pt_other, pg, pb, low,
    wb, wr, c2r, w2, c3r, gram_c, gram_p, gram_z, zw, qt,
    z_send, z_sem, link_send, xy_sem, core_send, core_sem, sends, b_sem, gc_sem, c1_sem,
    gp_sem, c2_sem, c3_sem, gz_sem, zw_sem, pz_sem, px_sem, pc_sem, ag_sem, agc_sem,
    local_sem, out_sem,
):
    dp, y = lax.axis_index("dp"), lax.axis_index("tensor")
    z, x, c = dp // 8, (dp // 2) % 4, dp % 2
    other = 1 - c
    replica = z // 4

    def device(dz=0, dx=0, dc=0, dy=0):
        return (((z + dz) % NZ) * 8 + ((x + dx) % NX) * 2 + (c + dc) % NC, (y + dy) % NY)

    sibling = device(dc=1)

    def remote(src, dst, send_sem, recv_sem, there):
        return pltpu.make_async_remote_copy(
            src_ref=src, dst_ref=dst, send_sem=send_sem, recv_sem=recv_sem,
            device_id=there, device_id_type=MESH,
        )

    def send(src, dst, send_sem, recv_sem, there):
        copy = remote(src, dst, send_sem, recv_sem, there)
        copy.start()
        return copy

    def arrived(ref, sem):
        remote(ref, ref, core_send.at[0], sem, sibling).wait_recv()

    def left(ref, sem):
        remote(ref, ref, sem, b_sem.at[0], sibling).wait_send()

    pending = []

    def later(ref, number):
        pending.append((ref, sends.at[number]))

    barrier = pltpu.get_barrier_semaphore()
    partners = [device(dz=d) for d in range(1, NZ)] + [sibling]
    partners += [
        device(dx=dx, dy=dy) for dx in range(NX) for dy in range(NY) if (dx, dy) != (0, 0)
    ]
    for partner in partners:
        pl.semaphore_signal(barrier, inc=1, device_id=partner, device_id_type=MESH)

    og_copy = pltpu.make_async_copy(og_hbm, og, local_sem.at[0])
    hid_copy = pltpu.make_async_copy(hid_hbm, hid, local_sem.at[1])
    q_copy = pltpu.make_async_copy(q_hbm, qv, local_sem.at[2])
    res_copy = pltpu.make_async_copy(res_hbm, res, local_sem.at[3])
    for copy in (og_copy, hid_copy, q_copy, res_copy):
        copy.start()

    og_copy.wait()
    total = jnp.zeros((48, 1024), F32)
    for g in range(4):
        pick = one_hot(iota((48, TOK_DEV), 0) == iota((48, TOK_DEV), 1) + g * TOK_DEV)
        lanes = [og[:, i * 512 + g * 128:i * 512 + (g + 1) * 128] for i in range(8)]
        total += dot(pick, jnp.concatenate(lanes, axis=1))
    for i in range(8):
        pack[i] = total[:, i * 128:(i + 1) * 128].astype(BF16)
    for h in range(NQ):
        zbuf[h * NZ + z] = pack[replica * NQ + h]

    pl.semaphore_wait(barrier, len(partners))

    def send_z(h):
        if h:
            left(zbuf.at[pl.ds(0, 7)], z_send.at[h - 1])
        for d in range(1, NZ):
            there = (z + d) % NZ // 4
            send(
                pack.at[there * NQ + h], zbuf.at[h * NZ + z], z_send.at[h], z_sem.at[h],
                device(dz=d),
            )

    send_z(0)

    hid_copy.wait()
    hidden = hid[...]
    for i in range(3):
        r = iota((1, 256), 1) + i * 256
        rx = jnp.where(r >= 192, 1, 0) + jnp.where(r >= 384, 1, 0) + jnp.where(r >= 576, 1, 0)
        r = r - rx * 192
        rc = jnp.where(r >= 96, 1, 0)
        r = r - rc * 96
        rz = div12(r)
        token = rz * 96 + rx * 24 + rc * 12 + (r - rz * 12)
        pick = one_hot(iota((TOK, 256), 0) == token)
        hid_t[:, i * 256:(i + 1) * 256] = dot(hidden, pick).astype(BF16)
    send_z(1)
    pacc[...] = jnp.zeros_like(pacc)
    res_copy.wait()
    q_copy.wait()

    def block(h, first, second, part=None, core=None):
        dx, dy = (first, second) if h % 2 == 0 else (second, first)
        row = (x + dx) % NX * 192 + (c if core is None else core) * 96
        count = 96
        if part is not None:
            row, count = row + 48 * part, 48
        return grads.at[(y + dy) % NY * NQ + h, pl.ds(pl.multiple_of(row, 16), count)]

    flights = [[] for _ in range(4)]

    def push(h, first, second, part, axis, step):
        link = link_of(h, axis, step)
        number = len(flights[link])
        if number >= DEEP:
            flights[link][number - DEEP].wait_send()
        there = device(dx=step) if link < 2 else device(dy=step)
        f, s = first, second
        if axis == 0:
            f = (first - step) % 4
        else:
            s = (second - step) % 4
        ref = block(h, first, second, part)
        flights[link].append(
            send(ref, ref, link_send.at[link, number % DEEP], xy_sem.at[h, f * 4 + s], there)
        )

    def share(h, first, second):
        ref = block(h, first, second)
        rel = second if h % 2 == 0 else first
        send(ref, ref, core_send.at[0], core_sem.at[h, rel], sibling)

    def begin(h):
        if h + 2 < NQ:
            send_z(h + 2)
        arrived(zbuf.at[pl.ds(0, 7)], z_sem.at[h])
        packed = zbuf[h * NZ:(h + 1) * NZ].reshape(384, 128)
        row = pl.multiple_of(x * 192 + c * 96, 16)
        for g in range(4):
            r, s = iota((96, 384), 0), iota((96, 384), 1)
            pick = one_hot(s == r + div12(r) * 36 + g * TOK_DEV)
            grads[y * NQ + h, pl.ds(row, 96), g * 128:(g + 1) * 128] = dot(pick, packed).astype(BF16)
        share(h, 0, 0)

    def forward(h, f, s):
        arrived(block(h, f, s), xy_sem.at[h, f * 4 + s])
        share(h, f, s)

    blocks_out = []

    def add_left(cols):
        pacc[...] += dot(qv[:, cols], mer[:, cols], ((1,), (1,)))

    def compute(h, rel):
        arrived(grads.at[0, pl.ds(0, 384)], core_sem.at[h, rel])
        yb = (y + rel) % NY
        base = pl.multiple_of(yb * 2048 + h * 512, 512)

        def tile(i, carry):
            col = pl.multiple_of(base + i * 256, 256)
            part = grads[yb * NQ + h, :, pl.ds(pl.multiple_of(i * 256, 256), 256)]
            merged = dot(hid_t[...], part) + res[:, pl.ds(col, 256)].astype(F32)
            mer[:, pl.ds(col, 256)] = merged.astype(BF16)
            return carry

        if blocks_out:
            add_left(blocks_out[-1])
        lax.fori_loop(0, 2, tile, 0, unroll=True)
        cols = pl.ds(base, 512)
        pltpu.make_async_copy(mer.at[:, cols], mer_out.at[:, cols], out_sem.at[0]).start()
        blocks_out.append(cols)

    steps = {"begin": begin, "forward": forward, "compute": compute, "push": push}
    for what, *where in ORDER:
        steps[what](*where)

    def end():
        for ref, sem in pending:
            left(ref, sem)
        left(zbuf.at[pl.ds(0, 7)], z_send.at[NQ - 1])
        for link in range(4):
            for copy in flights[link][-DEEP:]:
                copy.wait_send()
        left(grads.at[pl.ds(0, 8)], core_send.at[0])
        pltpu.make_async_copy(mer, mer_out, out_sem.at[0]).wait()

    add_left(blocks_out[-1])
    pt_mine[...] = jnp.zeros_like(pt_mine)
    pt_mine[:, 0:ROWS] = pacc[...]
    send(pt_mine, pt_other, sends.at[0], b_sem.at[0], device(dz=4))
    later(pt_mine, 0)
    arrived(pt_other, b_sem.at[0])
    pt = pt_mine[...] + pt_other[...]
    slot = c * 16 + z % 4 * 4 + x
    pg[slot] = pt

    gram = dot(pt, jnp.concatenate([pt, jnp.zeros((96, PAD), F32)], axis=0), ((1,), (1,)), HIGH)
    packed = gram[0:8]
    for g in range(1, 4):
        packed += pltpu.roll(gram[8 * g:8 * g + 8], 32 * g, 1)
    gram_c[0] = packed
    send(gram_c.at[0], gram_c.at[1], sends.at[1], gc_sem.at[0], sibling)
    later(gram_c.at[0], 1)
    for d in range(1, 4):
        send(pg.at[slot], pg.at[slot], sends.at[3], px_sem.at[0], device(dx=d))
    later(pg.at[pl.ds(0, 3)], 3)

    hi = pt.astype(BF16)
    rest = pt - hi.astype(F32)
    mid = rest.astype(BF16)
    rest = (rest - mid.astype(F32)).astype(BF16)
    terms = jnp.concatenate([hi, mid, rest], axis=0)[:, :ROWS]

    def w_tiles(first):
        def tile(i, carry):
            nb = first + i * 2
            col = pl.multiple_of(nb * 128, 256)
            product = dot(terms, mer[:, pl.ds(col, 256)])
            total = product[0:32] + (product[32:64] + product[64:96])
            wb[nb] = total[:, 0:128]
            wb[nb + 1] = total[:, 128:256]
            return carry

        lax.fori_loop(0, 8, tile, 0, unroll=4)

    for h in range(2):
        w_tiles(other * 32 + h * 16)
        send(
            wb.at[pl.ds(other * 32 + h * 16, 16)], wr.at[pl.ds(h * 16, 16)],
            sends.at[2], c1_sem.at[h], sibling,
        )
        if h:
            continue
        arrived(gram_c.at[0], gc_sem.at[0])
        spot = x * 4 + y
        gram_p[spot] = gram_c[0] + gram_c[1]
        for dx in range(NX):
            for dy in range(NY):
                if (dx, dy) != (0, 0):
                    send(
                        gram_p.at[spot], gram_p.at[spot], sends.at[4], gp_sem.at[0],
                        device(dx=dx, dy=dy),
                    )
        later(gram_p.at[pl.ds(0, 15)], 4)
    later(wr, 2)
    places = (x, y)

    for h in range(2):
        w_tiles(c * 32 + h * 16)
        arrived(wr.at[pl.ds(h * 16, 16)], c1_sem.at[h])
        at = pl.ds(c * 32 + h * 16, 16)
        wb[at] = wb[at] + wr[pl.ds(h * 16, 16)]
        for d in range(1, 4):
            there = (places[h] + d) % 4
            send(
                wb.at[pl.ds(c * 32 + h * 16 + there * 4, 4)], c2r.at[h * 4 + places[h]],
                sends.at[5], c2_sem.at[h], device(dx=d) if h == 0 else device(dy=d),
            )
    later(c2r.at[pl.ds(0, 6)], 5)

    arrived(gram_p.at[pl.ds(0, 15)], gp_sem.at[0])
    total = gram_p[0]
    for i in range(1, 16):
        total += gram_p[i]
    gram_z[z] = total
    for d in range(1, NZ):
        send(gram_z.at[z], gram_z.at[z], sends.at[9], gz_sem.at[0], device(dz=d))
    later(gram_z.at[pl.ds(0, 7)], 9)

    arrived(pg.at[pl.ds(0, 3)], px_sem.at[0])
    group = pg.at[pl.ds(c * 16 + z % 4 * 4, 4)]
    for d in (1, -1, 2):
        send(group, group, sends.at[8], pz_sem.at[0], device(dz=d))
    later(pg.at[pl.ds(0, 12)], 8)

    for h in range(2):
        arrived(c2r.at[pl.ds(0, 3)], c2_sem.at[h])
        total = wb[pl.ds(c * 32 + h * 16 + places[h] * 4, 4)]
        for d in range(1, 4):
            total += c2r[h * 4 + (places[h] + d) % 4]
        w2[h] = total
        for d in range(1, 4):
            there = (places[1 - h] + d) % 4
            send(
                w2.at[h, there], c3r.at[h * 4 + places[1 - h]],
                sends.at[7], c3_sem.at[h], device(dy=d) if h == 0 else device(dx=d),
            )
    later(c3r.at[pl.ds(0, 6)], 7)

    arrived(gram_z.at[pl.ds(0, 7)], gz_sem.at[0])
    total = gram_z[0]
    for i in range(1, NZ):
        total += gram_z[i]
    total = total * 0.5
    lane = iota((RANK, 128), 1)
    gram = jnp.concatenate(
        [total] + [pltpu.roll(total, 128 - 32 * g, 1) for g in range(1, 4)], axis=0
    )
    inverse = eliminate(jnp.where(lane < RANK, gram, 0.0))[:, 0:RANK]

    for h in range(2):
        arrived(c3r.at[pl.ds(0, 3)], c3_sem.at[h])
        total = w2[h, places[1 - h]]
        for d in range(1, 4):
            total += c3r[h * 4 + (places[1 - h] + d) % 4]
        zw[h * NZ + z] = (dot(inverse, total, precision=HIGH) * 0.5).astype(BF16)
        for d in range(1, NZ):
            send(zw.at[h * NZ + z], zw.at[h * NZ + z], sends.at[10], zw_sem.at[h], device(dz=d))
    later(zw.at[pl.ds(0, 14)], 10)

    mine = c * 16 + x * 4 + y
    for h in range(2):
        arrived(zw.at[pl.ds(0, 7)], zw_sem.at[h])
        total = zw[h * NZ].astype(F32)
        for i in range(1, NZ):
            total += zw[h * NZ + i].astype(F32)
        qt[h, mine] = total.astype(BF16)
        for dx in range(NX):
            for dy in range(NY):
                if (dx, dy) != (0, 0):
                    send(
                        qt.at[h, mine], qt.at[h, mine], sends.at[11 + h],
                        ag_sem.at[h * dx + h], device(dx=dx, dy=dy),
                    )
        later(qt.at[h, pl.ds(0, 15)], 11 + h)

    arrived(pg.at[pl.ds(0, 12)], pz_sem.at[0])
    half = pg.at[pl.ds(c * 16, 16)]
    send(half, half, sends.at[14], pc_sem.at[0], sibling)
    later(half, 14)
    own = dot(inverse, pg[slot], precision=HIGH)
    own = jnp.concatenate([own, jnp.zeros((96, PAD), F32)], axis=0).T
    low[...] = own[0:ROWS].astype(BF16)
    low_copy = pltpu.make_async_copy(low, low_out, local_sem.at[0])
    low_copy.start()
    arrived(half, pc_sem.at[0])
    for i in range(8):
        blocks = []
        for p in range(4 * i, 4 * i + 4):
            blocks.append(pg[p % 2 * 16 + p // 8 * 4 + p // 2 % 4][:, 0:ROWS])
        blocks = jnp.concatenate(blocks, axis=1)
        pb[:, i * 896:(i + 1) * 896] = dot(inverse, blocks, precision=HIGH)
    pb_copy = pltpu.make_async_copy(pb, pb_out, local_sem.at[1])
    pb_copy.start()

    arrived(qt.at[0, pl.ds(0, 15)], ag_sem.at[0])
    ours = qt.at[0, pl.ds(c * 16, 16)]
    send(ours, ours, sends.at[13], agc_sem.at[0], sibling)
    for dx in (0, 1, 3, 2):
        rows = qt.at[1, pl.ds(c * 16 + (x + 4 - dx) % 4 * 4, 4)]
        arrived(qt.at[1, pl.ds(0, 4 if dx else 3)], ag_sem.at[1 + dx])
        send(rows, rows, sends.at[13], agc_sem.at[0], sibling)
    later(qt.at[0], 13)
    arrived(qt.at[0], agc_sem.at[0])
    qt_copy = pltpu.make_async_copy(qt, qt_out, local_sem.at[2])
    qt_copy.start()
    end()
    low_copy.wait()
    pb_copy.wait()
    qt_copy.wait()


def exchange(
    hidden, out_grads, q_prev, residual,
):
    dma = pltpu.SemaphoreType.DMA
    any_spec = pl.BlockSpec(memory_space=pl.ANY)
    return pl.pallas_call(
        main_kernel,
        out_shape=(
            jax.ShapeDtypeStruct((ROWS, D), BF16),
            jax.ShapeDtypeStruct((RANK, 32 * ROWS), F32),
            jax.ShapeDtypeStruct((2, 32, RANK, 128), BF16),
            jax.ShapeDtypeStruct((ROWS, 128), BF16),
        ),
        in_specs=[any_spec] * 4,
        out_specs=(any_spec,) * 4,
        scratch_shapes=[
            pltpu.VMEM((ROWS, TOK), BF16),
            pltpu.VMEM((TOK_DEV, 4096), BF16),
            pltpu.VMEM((8, 48, 128), BF16),
            pltpu.VMEM((NQ * NZ, 48, 128), BF16),
            pltpu.VMEM((4 * NQ, TOK, 512), BF16),
            pltpu.VMEM((ROWS, TOK), BF16),
            pltpu.VMEM((ROWS, D), BF16),
            pltpu.VMEM((ROWS, D), BF16),
            pltpu.VMEM((RANK, D), BF16),
            pltpu.VMEM((RANK, ROWS), F32),
            pltpu.VMEM((RANK, PAD), F32),
            pltpu.VMEM((RANK, PAD), F32),
            pltpu.VMEM((32, RANK, PAD), F32),
            pltpu.VMEM((RANK, 32 * ROWS), F32),
            pltpu.VMEM((ROWS, 128), BF16),
            pltpu.VMEM((64, RANK, 128), F32),
            pltpu.VMEM((32, RANK, 128), F32),
            pltpu.VMEM((8, 4, RANK, 128), F32),
            pltpu.VMEM((2, 4, RANK, 128), F32),
            pltpu.VMEM((8, RANK, 128), F32),
            pltpu.VMEM((2, 8, 128), F32),
            pltpu.VMEM((16, 8, 128), F32),
            pltpu.VMEM((NZ, 8, 128), F32),
            pltpu.VMEM((2 * NZ, RANK, 128), BF16),
            pltpu.VMEM((2, 32, RANK, 128), BF16),
            dma((NQ,)),
            dma((NQ,)),
            dma((4, DEEP)),
            dma((NQ, 16)),
            dma((1,)),
            dma((NQ, 4)),
            dma((15,)),
            dma((1,)),
            dma((1,)),
            dma((2,)),
            dma((1,)),
            dma((2,)),
            dma((2,)),
            dma((1,)),
            dma((2,)),
            dma((1,)),
            dma((1,)),
            dma((1,)),
            dma((5,)),
            dma((1,)),
            dma((4,)),
            dma((1,)),
        ],
        name="exchange",
        compiler_params=pltpu.CompilerParams(
            collective_id=0, has_side_effects=True, vmem_limit_bytes=60 * 2**20
        ),
    )(hidden, out_grads, q_prev, residual)


def final_kernel(
    mer_hbm, pb_hbm, qt_hbm, low_hbm, res_hbm, p_hbm, q_hbm,
    mer, res, qt, low, q_new, pb, in_sem, out_sem,
):
    low_copy = pltpu.make_async_copy(low_hbm, low, in_sem.at[0])
    qt_copy = pltpu.make_async_copy(qt_hbm, qt, in_sem.at[1])
    p_copy = pltpu.make_async_copy(pb_hbm, pb, in_sem.at[2])
    low_copy.start()
    qt_copy.start()
    pieces = []
    for i in range(4):
        cols = pl.ds(i * 2048, 2048)
        pieces.append(pltpu.make_async_copy(mer_hbm.at[:, cols], mer.at[:, cols], in_sem.at[3 + i]))
        pieces[-1].start()
    p_copy.start()

    def place(nb):
        core, part, v = nb // 32, nb % 32 // 16, nb % 16
        return part, core * 16 + (v if part == 0 else v % 4 * 4 + v // 4)

    low_copy.wait()
    qt_copy.wait()
    p_low = low[:, 0:RANK]
    for i in range(4):
        pieces[i].wait()
        for nb in range(i * 16, i * 16 + 16, 2):
            q_low = jnp.concatenate([qt[place(nb)], qt[place(nb + 1)]], axis=1)
            cols = slice(nb * 128, nb * 128 + 256)
            res[:, cols] = (mer[:, cols].astype(F32) - dot(p_low, q_low)).astype(BF16)
        cols = pl.ds(i * 2048, 2048)
        pltpu.make_async_copy(res.at[:, cols], res_hbm.at[:, cols], out_sem.at[0]).start()
        if i == 0:
            p_copy.wait()
            p_copy = pltpu.make_async_copy(pb, p_hbm, in_sem.at[2])
            p_copy.start()

    nb = lax.axis_index("dp")
    part, v = nb % 32 // 16, nb % 16
    slot = nb // 32 * 16 + jnp.where(part == 0, v, v % 4 * 4 + v // 4)
    q_new[...] = qt[part, slot].astype(F32)
    q_copy = pltpu.make_async_copy(q_new, q_hbm, in_sem.at[0])
    q_copy.start()
    q_copy.wait()
    p_copy.wait()
    pltpu.make_async_copy(res, res_hbm, out_sem.at[0]).wait()


def finish(mer, pb, qt, low):
    any_spec = pl.BlockSpec(memory_space=pl.ANY)
    return pl.pallas_call(
        final_kernel,
        out_shape=(
            jax.ShapeDtypeStruct((ROWS, D), BF16),
            jax.ShapeDtypeStruct((RANK, 32 * ROWS), F32),
            jax.ShapeDtypeStruct((RANK, 128), F32),
        ),
        in_specs=[any_spec] * 4,
        out_specs=(any_spec,) * 3,
        scratch_shapes=[
            pltpu.VMEM((ROWS, D), BF16),
            pltpu.VMEM((ROWS, D), BF16),
            pltpu.VMEM((2, 32, RANK, 128), BF16),
            pltpu.VMEM((ROWS, 128), BF16),
            pltpu.VMEM((RANK, 128), F32),
            pltpu.VMEM((RANK, 32 * ROWS), F32),
            pltpu.SemaphoreType.DMA((7,)),
            pltpu.SemaphoreType.DMA((1,)),
        ],
        name="finish",
        compiler_params=pltpu.CompilerParams(vmem_limit_bytes=60 * 2**20),
    )(mer, pb, qt, low)


def on_device(hidden_acts, out_grads, residual_in, q_prev):
    parts = exchange(hidden_acts[0].T, out_grads, q_prev.T, residual_in[0])
    residual_out, p_basis, q_new = finish(*parts)
    return p_basis.T, q_new.T, residual_out[None]


def solution(mesh):
    in_specs = (P("dp", None, "tensor"), P("dp", "tensor"), P("dp", "tensor", None), P())
    out_specs = (P("tensor", None), P("dp", None), P("dp", "tensor", None))
    return jax.shard_map(
        on_device, mesh=mesh, in_specs=in_specs, out_specs=out_specs, check_vma=False
    )
```

```python
import jax
import jax.numpy as jnp
from jax import lax
from jax.experimental import pallas as pl
from jax.experimental.pallas import tpu as pltpu
from jax.sharding import PartitionSpec as P

NZ, NX, NC, NY = 8, 4, 2, 4
RANK = 32
TOK, TOK_DEV = 768, 12
ROWS = 224
D = 8192
PAD = 256
NQ = 4
DEEP = 2
PLANE = sorted(
    [(dx, dy) for dx in range(NX) for dy in range(NY) if (dx, dy) != (0, 0)],
    key=lambda o: -min(o[0], NX - o[0]) - min(o[1], NY - o[1]),
)
ALONG_Z = (4, 3, 5, 2, 6, 1, 7)
F32, BF16 = jnp.float32, jnp.bfloat16
HIGH = lax.Precision.HIGHEST
MESH = pl.DeviceIdType.MESH


def link_of(h, axis, step):
    return 2 * ((axis + h) % 2) + (0 if step == 1 else 1)


def plan():
    hop, lat, core_lat, work = 2.1, 2.8, 1.6, 0.65
    now, count, order, arrivals = 0.0, 0, [], []
    parts, both = {}, {}
    queue, done, free = [[] for _ in range(4)], [[] for _ in range(4)], [0.0] * 4
    starts = [(4.6 + 2.1 * h, h) for h in range(NQ)]
    todo = [(h, rel) for h in range(NQ) for rel in (0, 3, 1, 2)]

    def put(kind, size, key, push):
        nonlocal count
        count += 1
        queue[link_of(push[0], push[4], push[5])].append(((kind, push[0], count), size, key, push))

    def spread(h, f):
        put(2, 1.0, (h, f, 3), (h, f, 0, None, 1, 1))
        put(2, 1.0, (h, f, 1), (h, f, 0, None, 1, -1))

    while len(order) < NQ * 40:
        arrivals.sort()
        if starts and starts[0][0] <= now:
            h = starts.pop(0)[1]
            order.append(("begin", h))
            now += 0.3
            put(0, 1.0, (h, 3, 0), (h, 0, 0, None, 0, 1))
            put(0, 1.0, (h, 1, 0), (h, 0, 0, None, 0, -1))
            spread(h, 0)
            both[h, 0, 0] = now + core_lat
            continue
        if arrivals and arrivals[0][0] <= now:
            h, f, s = arrivals.pop(0)[1]
            if f == 2 and s == 0 or s == 2:
                parts[h, f, s] = parts.get((h, f, s), 0) + 1
                if parts[h, f, s] < 2:
                    continue
            order.append(("forward", h, f, s))
            if s == 0:
                if f != 2:
                    step = 1 if f == 3 else -1
                    put(1, 0.5, (h, 2, 0), (h, f, 0, 0 if f == 3 else 1, 0, step))
                spread(h, f)
            elif s != 2:
                step = 1 if s == 3 else -1
                put(3, 0.5, (h, f, 2), (h, f, s, 0 if s == 3 else 1, 1, step))
            both[h, f, s] = now + core_lat
            now += 0.08
            continue
        sent = False
        for link in range(4):
            if queue[link] and (len(done[link]) < DEEP or done[link][-DEEP] <= now):
                queue[link].sort()
                _, size, key, push = queue[link].pop(0)
                free[link] = max(now, free[link]) + size * hop
                done[link].append(free[link])
                arrivals.append((free[link] + lat, key))
                order.append(("push",) + push)
                now += 0.04
                sent = True
                break
        if sent:
            continue
        ready = None
        for h, rel in todo:
            need = [(h, i, rel) if h % 2 == 0 else (h, rel, i) for i in range(4)]
            if all(both.get(k, 1e9) <= now for k in need):
                ready = (h, rel)
                break
        if ready:
            todo.remove(ready)
            order.append(("compute",) + ready)
            now += work
            continue
        times = [t for t, _ in arrivals[:1]] + [t for t, _ in starts[:1]]
        times += [t for t in both.values() if t > now]
        times += [
            done[link][-DEEP] for link in range(4)
            if queue[link] and len(done[link]) >= DEEP and done[link][-DEEP] > now
        ]
        now = max(now + 1e-3, min(times))
    return order


ORDER = plan()


def iota(shape, axis):
    return lax.broadcasted_iota(jnp.int32, shape, axis)


def div12(v):
    return (v * 5462) >> 16


def one_hot(cond):
    return jnp.where(cond, 1.0, 0.0).astype(BF16)


def dot(a, b, dims=((1,), (0,)), precision=None):
    return lax.dot_general(
        a, b, (dims, ((), ())), precision=precision, preferred_element_type=F32
    )


def eliminate(gram):
    row, lane = iota((RANK, 128), 0), iota((RANK, 128), 1)
    work = gram + jnp.where(lane == row + RANK, 1.0, 0.0)
    for k in range(RANK):
        column = jnp.broadcast_to(work[:, k:k + 1], (RANK, 128))
        scale = lax.rsqrt(column[k:k + 1, :])
        pivot_row = work[k:k + 1, :] * scale
        below = work - (column * scale) * pivot_row
        work = jnp.where(row > k, below, jnp.where(row == k, pivot_row, work))
    inverse = pltpu.roll(work, 128 - RANK, 1)
    return jnp.where(lane < RANK, inverse, 0.0)


def main_kernel(
    hid_hbm, og_hbm, q_hbm, res_hbm,
    mer_out, pb_out, qt_out, low_out,
    hid, og, pack, zbuf, grads, hid_t, res, mer, qv, pacc, pt_mine, pt_other, pg, pb, low,
    wb, wr, c2r, w2, c3r, gram_c, gram_p, gram_z, zw, qt,
    z_send, z_sem, link_send, xy_sem, core_send, core_sem, sends, b_sem, gc_sem, c1_sem,
    gp_sem, c2_sem, c3_sem, gz_sem, zw_sem, pz_sem, px_sem, pc_sem, ag_sem, agc_sem,
    local_sem, out_sem,
):
    dp, y = lax.axis_index("dp"), lax.axis_index("tensor")
    z, x, c = dp // 8, (dp // 2) % 4, dp % 2
    other = 1 - c
    replica = z // 4

    def device(dz=0, dx=0, dc=0, dy=0):
        return (((z + dz) % NZ) * 8 + ((x + dx) % NX) * 2 + (c + dc) % NC, (y + dy) % NY)

    sibling = device(dc=1)

    def remote(src, dst, send_sem, recv_sem, there):
        return pltpu.make_async_remote_copy(
            src_ref=src, dst_ref=dst, send_sem=send_sem, recv_sem=recv_sem,
            device_id=there, device_id_type=MESH,
        )

    def send(src, dst, send_sem, recv_sem, there):
        copy = remote(src, dst, send_sem, recv_sem, there)
        copy.start()
        return copy

    def arrived(ref, sem):
        remote(ref, ref, core_send.at[0], sem, sibling).wait_recv()

    def left(ref, sem):
        remote(ref, ref, sem, b_sem.at[0], sibling).wait_send()

    pending = []

    def later(ref, number):
        pending.append((ref, sends.at[number]))

    barrier = pltpu.get_barrier_semaphore()
    partners = [device(dz=d) for d in range(1, NZ)] + [sibling]
    partners += [
        device(dx=dx, dy=dy) for dx in range(NX) for dy in range(NY) if (dx, dy) != (0, 0)
    ]
    for partner in partners:
        pl.semaphore_signal(barrier, inc=1, device_id=partner, device_id_type=MESH)

    og_copy = pltpu.make_async_copy(og_hbm, og, local_sem.at[0])
    hid_copy = pltpu.make_async_copy(hid_hbm, hid, local_sem.at[1])
    q_copy = pltpu.make_async_copy(q_hbm, qv, local_sem.at[2])
    res_copy = pltpu.make_async_copy(res_hbm, res, local_sem.at[3])
    for copy in (og_copy, hid_copy, q_copy, res_copy):
        copy.start()

    og_copy.wait()
    total = jnp.zeros((48, 1024), F32)
    for g in range(4):
        pick = one_hot(iota((48, TOK_DEV), 0) == iota((48, TOK_DEV), 1) + g * TOK_DEV)
        lanes = [og[:, i * 512 + g * 128:i * 512 + (g + 1) * 128] for i in range(8)]
        total += dot(pick, jnp.concatenate(lanes, axis=1))
    for i in range(8):
        pack[i] = total[:, i * 128:(i + 1) * 128].astype(BF16)
    for h in range(NQ):
        zbuf[h * NZ + z] = pack[replica * NQ + h]

    pl.semaphore_wait(barrier, len(partners))

    def send_z(h):
        if h:
            left(zbuf.at[pl.ds(0, 7)], z_send.at[h - 1])
        for d in ALONG_Z:
            there = (z + d) % NZ // 4
            send(
                pack.at[there * NQ + h], zbuf.at[h * NZ + z], z_send.at[h], z_sem.at[h],
                device(dz=d),
            )

    send_z(0)

    hid_copy.wait()
    hidden = hid[...]
    for i in range(3):
        r = iota((1, 256), 1) + i * 256
        rx = jnp.where(r >= 192, 1, 0) + jnp.where(r >= 384, 1, 0) + jnp.where(r >= 576, 1, 0)
        r = r - rx * 192
        rc = jnp.where(r >= 96, 1, 0)
        r = r - rc * 96
        rz = div12(r)
        token = rz * 96 + rx * 24 + rc * 12 + (r - rz * 12)
        pick = one_hot(iota((TOK, 256), 0) == token)
        hid_t[:, i * 256:(i + 1) * 256] = dot(hidden, pick).astype(BF16)
    send_z(1)
    pacc[...] = jnp.zeros_like(pacc)
    pt_mine[...] = jnp.zeros_like(pt_mine)
    res_copy.wait()
    q_copy.wait()

    def block(h, first, second, part=None, core=None):
        dx, dy = (first, second) if h % 2 == 0 else (second, first)
        row = (x + dx) % NX * 192 + (c if core is None else core) * 96
        count = 96
        if part is not None:
            row, count = row + 48 * part, 48
        return grads.at[(y + dy) % NY * NQ + h, pl.ds(pl.multiple_of(row, 16), count)]

    flights = [[] for _ in range(4)]

    def push(h, first, second, part, axis, step):
        link = link_of(h, axis, step)
        number = len(flights[link])
        if number >= DEEP:
            flights[link][number - DEEP].wait_send()
        there = device(dx=step) if link < 2 else device(dy=step)
        f, s = first, second
        if axis == 0:
            f = (first - step) % 4
        else:
            s = (second - step) % 4
        ref = block(h, first, second, part)
        flights[link].append(
            send(ref, ref, link_send.at[link, number % DEEP], xy_sem.at[h, f * 4 + s], there)
        )

    def share(h, first, second):
        ref = block(h, first, second)
        rel = second if h % 2 == 0 else first
        send(ref, ref, core_send.at[0], core_sem.at[h, rel], sibling)

    def begin(h):
        if h + 2 < NQ:
            send_z(h + 2)
        arrived(zbuf.at[pl.ds(0, 7)], z_sem.at[h])
        packed = zbuf[h * NZ:(h + 1) * NZ].reshape(384, 128)
        row = pl.multiple_of(x * 192 + c * 96, 16)
        for g in range(4):
            r, s = iota((96, 384), 0), iota((96, 384), 1)
            pick = one_hot(s == r + div12(r) * 36 + g * TOK_DEV)
            grads[y * NQ + h, pl.ds(row, 96), g * 128:(g + 1) * 128] = dot(pick, packed).astype(BF16)
        share(h, 0, 0)

    def forward(h, f, s):
        arrived(block(h, f, s), xy_sem.at[h, f * 4 + s])
        share(h, f, s)

    blocks_out = []

    def add_left(cols):
        pacc[...] += dot(qv[:, cols], mer[:, cols], ((1,), (1,)))

    def compute(h, rel):
        arrived(grads.at[0, pl.ds(0, 384)], core_sem.at[h, rel])
        yb = (y + rel) % NY
        base = pl.multiple_of(yb * 2048 + h * 512, 512)

        def tile(i, carry):
            col = pl.multiple_of(base + i * 256, 256)
            part = grads[yb * NQ + h, :, pl.ds(pl.multiple_of(i * 256, 256), 256)]
            merged = dot(hid_t[...], part) + res[:, pl.ds(col, 256)].astype(F32)
            mer[:, pl.ds(col, 256)] = merged.astype(BF16)
            return carry

        if blocks_out:
            add_left(blocks_out[-1])
        lax.fori_loop(0, 2, tile, 0, unroll=True)
        cols = pl.ds(base, 512)
        pltpu.make_async_copy(mer.at[:, cols], mer_out.at[:, cols], out_sem.at[0]).start()
        blocks_out.append(cols)

    steps = {"begin": begin, "forward": forward, "compute": compute, "push": push}
    for what, *where in ORDER:
        steps[what](*where)

    def end():
        for ref, sem in pending:
            left(ref, sem)
        left(zbuf.at[pl.ds(0, 7)], z_send.at[NQ - 1])
        for link in range(4):
            for copy in flights[link][-DEEP:]:
                copy.wait_send()
        left(grads.at[pl.ds(0, 8)], core_send.at[0])
        pltpu.make_async_copy(mer, mer_out, out_sem.at[0]).wait()

    add_left(blocks_out[-1])
    pt_mine[:, 0:ROWS] = pacc[...]
    send(pt_mine, pt_other, sends.at[0], b_sem.at[0], device(dz=4))
    later(pt_mine, 0)
    arrived(pt_other, b_sem.at[0])
    pt = pt_mine[...] + pt_other[...]
    slot = c * 16 + z % 4 * 4 + x
    pg[slot] = pt

    gram = dot(pt, jnp.concatenate([pt, jnp.zeros((96, PAD), F32)], axis=0), ((1,), (1,)), HIGH)
    packed = gram[0:8]
    for g in range(1, 4):
        packed += pltpu.roll(gram[8 * g:8 * g + 8], 32 * g, 1)
    gram_c[0] = packed
    send(gram_c.at[0], gram_c.at[1], sends.at[1], gc_sem.at[0], sibling)
    later(gram_c.at[0], 1)

    hi = pt.astype(BF16)
    rest = pt - hi.astype(F32)
    mid = rest.astype(BF16)
    rest = (rest - mid.astype(F32)).astype(BF16)
    terms = jnp.concatenate([hi, mid, rest], axis=0)[:, :ROWS]

    def w_tiles(first):
        def tile(i, carry):
            nb = first + i * 2
            col = pl.multiple_of(nb * 128, 256)
            product = dot(terms, mer[:, pl.ds(col, 256)])
            total = product[0:32] + (product[32:64] + product[64:96])
            wb[nb] = total[:, 0:128]
            wb[nb + 1] = total[:, 128:256]
            return carry

        lax.fori_loop(0, 8, tile, 0, unroll=True)

    for h in range(2):
        w_tiles(other * 32 + h * 16)
        send(
            wb.at[pl.ds(other * 32 + h * 16, 16)], wr.at[pl.ds(h * 16, 16)],
            sends.at[2], c1_sem.at[h], sibling,
        )
        if h:
            continue
        for d in range(1, 4):
            send(pg.at[slot], pg.at[slot], sends.at[3], px_sem.at[0], device(dx=d))
        later(pg.at[pl.ds(0, 3)], 3)
        arrived(gram_c.at[0], gc_sem.at[0])
        spot = x * 4 + y
        gram_p[spot] = gram_c[0] + gram_c[1]
        for dx, dy in PLANE:
            send(
                gram_p.at[spot], gram_p.at[spot], sends.at[4], gp_sem.at[0],
                device(dx=dx, dy=dy),
            )
        later(gram_p.at[pl.ds(0, 15)], 4)
    later(wr, 2)
    places = (x, y)

    for h in range(2):
        w_tiles(c * 32 + h * 16)
        arrived(wr.at[pl.ds(h * 16, 16)], c1_sem.at[h])
        at = pl.ds(c * 32 + h * 16, 16)
        wb[at] = wb[at] + wr[pl.ds(h * 16, 16)]
        for d in (2, 1, 3):
            there = (places[h] + d) % 4
            send(
                wb.at[pl.ds(c * 32 + h * 16 + there * 4, 4)], c2r.at[h * 4 + places[h]],
                sends.at[5], c2_sem.at[h], device(dx=d) if h == 0 else device(dy=d),
            )
    later(c2r.at[pl.ds(0, 6)], 5)

    arrived(gram_p.at[pl.ds(0, 15)], gp_sem.at[0])
    total = gram_p[0]
    for i in range(1, 16):
        total += gram_p[i]
    gram_z[z] = total
    for d in ALONG_Z:
        send(gram_z.at[z], gram_z.at[z], sends.at[9], gz_sem.at[0], device(dz=d))
    later(gram_z.at[pl.ds(0, 7)], 9)

    arrived(pg.at[pl.ds(0, 3)], px_sem.at[0])
    group = pg.at[pl.ds(c * 16 + z % 4 * 4, 4)]
    for d in (1, -1, 2):
        send(group, group, sends.at[8], pz_sem.at[0], device(dz=d))
    later(pg.at[pl.ds(0, 12)], 8)

    for h in range(2):
        arrived(c2r.at[pl.ds(0, 3)], c2_sem.at[h])
        total = wb[pl.ds(c * 32 + h * 16 + places[h] * 4, 4)]
        for d in range(1, 4):
            total += c2r[h * 4 + (places[h] + d) % 4]
        w2[h] = total
        for d in (2, 1, 3):
            there = (places[1 - h] + d) % 4
            send(
                w2.at[h, there], c3r.at[h * 4 + places[1 - h]],
                sends.at[7], c3_sem.at[h], device(dy=d) if h == 0 else device(dx=d),
            )
    later(c3r.at[pl.ds(0, 6)], 7)

    arrived(gram_z.at[pl.ds(0, 7)], gz_sem.at[0])
    total = gram_z[0]
    for i in range(1, NZ):
        total += gram_z[i]
    total = total * 0.5
    lane = iota((RANK, 128), 1)
    gram = jnp.concatenate(
        [total] + [pltpu.roll(total, 128 - 32 * g, 1) for g in range(1, 4)], axis=0
    )
    inverse = eliminate(jnp.where(lane < RANK, gram, 0.0))[:, 0:RANK]

    for h in range(2):
        arrived(c3r.at[pl.ds(0, 3)], c3_sem.at[h])
        total = w2[h, places[1 - h]]
        for d in range(1, 4):
            total += c3r[h * 4 + (places[1 - h] + d) % 4]
        zw[h * NZ + z] = (dot(inverse, total, precision=HIGH) * 0.5).astype(BF16)
        for d in ALONG_Z:
            send(zw.at[h * NZ + z], zw.at[h * NZ + z], sends.at[10], zw_sem.at[h], device(dz=d))
    later(zw.at[pl.ds(0, 14)], 10)

    mine = c * 16 + x * 4 + y
    for h in range(2):
        arrived(zw.at[pl.ds(0, 7)], zw_sem.at[h])
        total = zw[h * NZ].astype(F32)
        for i in range(1, NZ):
            total += zw[h * NZ + i].astype(F32)
        qt[h, mine] = total.astype(BF16)
        for dx, dy in PLANE:
            send(
                qt.at[h, mine], qt.at[h, mine], sends.at[11 + h],
                ag_sem.at[h * dx + h], device(dx=dx, dy=dy),
            )
        later(qt.at[h, pl.ds(0, 15)], 11 + h)

    arrived(pg.at[pl.ds(0, 12)], pz_sem.at[0])
    half = pg.at[pl.ds(c * 16, 16)]
    send(half, half, sends.at[14], pc_sem.at[0], sibling)
    later(half, 14)
    own = dot(inverse, pg[slot], precision=HIGH)
    own = jnp.concatenate([own, jnp.zeros((96, PAD), F32)], axis=0).T
    low[...] = own[0:ROWS].astype(BF16)
    low_copy = pltpu.make_async_copy(low, low_out, local_sem.at[0])
    low_copy.start()
    arrived(half, pc_sem.at[0])
    for i in range(8):
        blocks = []
        for p in range(4 * i, 4 * i + 4):
            blocks.append(pg[p % 2 * 16 + p // 8 * 4 + p // 2 % 4][:, 0:ROWS])
        blocks = jnp.concatenate(blocks, axis=1)
        pb[:, i * 896:(i + 1) * 896] = dot(inverse, blocks, precision=HIGH)
    pb_copy = pltpu.make_async_copy(pb, pb_out, local_sem.at[1])
    pb_copy.start()

    arrived(qt.at[0, pl.ds(0, 15)], ag_sem.at[0])
    ours = qt.at[0, pl.ds(c * 16, 16)]
    send(ours, ours, sends.at[13], agc_sem.at[0], sibling)
    for dx in (0, 1, 3, 2):
        rows = qt.at[1, pl.ds(c * 16 + (x + 4 - dx) % 4 * 4, 4)]
        arrived(qt.at[1, pl.ds(0, 4 if dx else 3)], ag_sem.at[1 + dx])
        send(rows, rows, sends.at[13], agc_sem.at[0], sibling)
    later(qt.at[0], 13)
    arrived(qt.at[0], agc_sem.at[0])
    qt_copy = pltpu.make_async_copy(qt, qt_out, local_sem.at[2])
    qt_copy.start()
    end()
    low_copy.wait()
    pb_copy.wait()
    qt_copy.wait()


def exchange(
    hidden, out_grads, q_prev, residual,
):
    dma = pltpu.SemaphoreType.DMA
    any_spec = pl.BlockSpec(memory_space=pl.ANY)
    return pl.pallas_call(
        main_kernel,
        out_shape=(
            jax.ShapeDtypeStruct((ROWS, D), BF16),
            jax.ShapeDtypeStruct((RANK, 32 * ROWS), F32),
            jax.ShapeDtypeStruct((2, 32, RANK, 128), BF16),
            jax.ShapeDtypeStruct((ROWS, 128), BF16),
        ),
        in_specs=[any_spec] * 4,
        out_specs=(any_spec,) * 4,
        scratch_shapes=[
            pltpu.VMEM((ROWS, TOK), BF16),
            pltpu.VMEM((TOK_DEV, 4096), BF16),
            pltpu.VMEM((8, 48, 128), BF16),
            pltpu.VMEM((NQ * NZ, 48, 128), BF16),
            pltpu.VMEM((4 * NQ, TOK, 512), BF16),
            pltpu.VMEM((ROWS, TOK), BF16),
            pltpu.VMEM((ROWS, D), BF16),
            pltpu.VMEM((ROWS, D), BF16),
            pltpu.VMEM((RANK, D), BF16),
            pltpu.VMEM((RANK, ROWS), F32),
            pltpu.VMEM((RANK, PAD), F32),
            pltpu.VMEM((RANK, PAD), F32),
            pltpu.VMEM((32, RANK, PAD), F32),
            pltpu.VMEM((RANK, 32 * ROWS), F32),
            pltpu.VMEM((ROWS, 128), BF16),
            pltpu.VMEM((64, RANK, 128), F32),
            pltpu.VMEM((32, RANK, 128), F32),
            pltpu.VMEM((8, 4, RANK, 128), F32),
            pltpu.VMEM((2, 4, RANK, 128), F32),
            pltpu.VMEM((8, RANK, 128), F32),
            pltpu.VMEM((2, 8, 128), F32),
            pltpu.VMEM((16, 8, 128), F32),
            pltpu.VMEM((NZ, 8, 128), F32),
            pltpu.VMEM((2 * NZ, RANK, 128), BF16),
            pltpu.VMEM((2, 32, RANK, 128), BF16),
            dma((NQ,)),
            dma((NQ,)),
            dma((4, DEEP)),
            dma((NQ, 16)),
            dma((1,)),
            dma((NQ, 4)),
            dma((15,)),
            dma((1,)),
            dma((1,)),
            dma((2,)),
            dma((1,)),
            dma((2,)),
            dma((2,)),
            dma((1,)),
            dma((2,)),
            dma((1,)),
            dma((1,)),
            dma((1,)),
            dma((5,)),
            dma((1,)),
            dma((4,)),
            dma((1,)),
        ],
        name="exchange",
        compiler_params=pltpu.CompilerParams(
            collective_id=0, has_side_effects=True, vmem_limit_bytes=60 * 2**20
        ),
    )(hidden, out_grads, q_prev, residual)


def final_kernel(
    mer_hbm, pb_hbm, qt_hbm, low_hbm, res_hbm, p_hbm, q_hbm,
    mer, res, qt, low, q_new, pb, in_sem, out_sem,
):
    low_copy = pltpu.make_async_copy(low_hbm, low, in_sem.at[0])
    qt_copy = pltpu.make_async_copy(qt_hbm, qt, in_sem.at[1])
    p_copy = pltpu.make_async_copy(pb_hbm, pb, in_sem.at[2])
    low_copy.start()
    qt_copy.start()
    pieces = []
    for i in range(4):
        cols = pl.ds(i * 2048, 2048)
        pieces.append(pltpu.make_async_copy(mer_hbm.at[:, cols], mer.at[:, cols], in_sem.at[3 + i]))
        pieces[-1].start()
    p_copy.start()

    def place(nb):
        core, part, v = nb // 32, nb % 32 // 16, nb % 16
        return part, core * 16 + (v if part == 0 else v % 4 * 4 + v // 4)

    low_copy.wait()
    qt_copy.wait()
    p_low = low[:, 0:RANK]
    for i in range(4):
        pieces[i].wait()
        for nb in range(i * 16, i * 16 + 16, 2):
            q_low = jnp.concatenate([qt[place(nb)], qt[place(nb + 1)]], axis=1)
            cols = slice(nb * 128, nb * 128 + 256)
            res[:, cols] = (mer[:, cols].astype(F32) - dot(p_low, q_low)).astype(BF16)
        cols = pl.ds(i * 2048, 2048)
        pltpu.make_async_copy(res.at[:, cols], res_hbm.at[:, cols], out_sem.at[0]).start()
        if i == 0:
            p_copy.wait()
            p_copy = pltpu.make_async_copy(pb, p_hbm, in_sem.at[2])
            p_copy.start()

    nb = lax.axis_index("dp")
    part, v = nb % 32 // 16, nb % 16
    slot = nb // 32 * 16 + jnp.where(part == 0, v, v % 4 * 4 + v // 4)
    q_new[...] = qt[part, slot].astype(F32)
    q_copy = pltpu.make_async_copy(q_new, q_hbm, in_sem.at[0])
    q_copy.start()
    q_copy.wait()
    p_copy.wait()
    pltpu.make_async_copy(res, res_hbm, out_sem.at[0]).wait()


def finish(mer, pb, qt, low):
    any_spec = pl.BlockSpec(memory_space=pl.ANY)
    return pl.pallas_call(
        final_kernel,
        out_shape=(
            jax.ShapeDtypeStruct((ROWS, D), BF16),
            jax.ShapeDtypeStruct((RANK, 32 * ROWS), F32),
            jax.ShapeDtypeStruct((RANK, 128), F32),
        ),
        in_specs=[any_spec] * 4,
        out_specs=(any_spec,) * 3,
        scratch_shapes=[
            pltpu.VMEM((ROWS, D), BF16),
            pltpu.VMEM((ROWS, D), BF16),
            pltpu.VMEM((2, 32, RANK, 128), BF16),
            pltpu.VMEM((ROWS, 128), BF16),
            pltpu.VMEM((RANK, 128), F32),
            pltpu.VMEM((RANK, 32 * ROWS), F32),
            pltpu.SemaphoreType.DMA((7,)),
            pltpu.SemaphoreType.DMA((1,)),
        ],
        name="finish",
        compiler_params=pltpu.CompilerParams(vmem_limit_bytes=60 * 2**20),
    )(mer, pb, qt, low)


def on_device(hidden_acts, out_grads, residual_in, q_prev):
    parts = exchange(hidden_acts[0].T, out_grads, q_prev.T, residual_in[0])
    residual_out, p_basis, q_new = finish(*parts)
    return p_basis.T, q_new.T, residual_out[None]


def solution(mesh):
    in_specs = (P("dp", None, "tensor"), P("dp", "tensor"), P("dp", "tensor", None), P())
    out_specs = (P("tensor", None), P("dp", None), P("dp", "tensor", None))
    return jax.shard_map(
        on_device, mesh=mesh, in_specs=in_specs, out_specs=out_specs, check_vma=False
    )
```

```python
import jax
import jax.numpy as jnp
from jax import lax
from jax.experimental import pallas as pl
from jax.experimental.pallas import tpu as pltpu
from jax.sharding import PartitionSpec as P

NZ, NX, NC, NY = 8, 4, 2, 4
RANK = 32
TOK, TOK_DEV = 768, 12
ROWS = 224
D = 8192
PAD = 256
NQ = 4
DEEP = 2
PLANE = sorted(
    [(dx, dy) for dx in range(NX) for dy in range(NY) if (dx, dy) != (0, 0)],
    key=lambda o: -min(o[0], NX - o[0]) - min(o[1], NY - o[1]),
)
ALONG_Z = (4, 3, 5, 2, 6, 1, 7)
F32, BF16 = jnp.float32, jnp.bfloat16
HIGH = lax.Precision.HIGHEST
MESH = pl.DeviceIdType.MESH


def link_of(h, axis, step):
    return 2 * ((axis + h) % 2) + (0 if step == 1 else 1)


def plan():
    hop, lat, core_lat, work = 2.1, 2.8, 1.6, 0.65
    now, count, order, arrivals = 0.0, 0, [], []
    parts, both = {}, {}
    queue, done, free = [[] for _ in range(4)], [[] for _ in range(4)], [0.0] * 4
    starts = [(4.6 + 2.1 * h, h) for h in range(NQ)]
    todo = [(h, rel) for h in range(NQ) for rel in (0, 3, 1, 2)]

    def put(kind, size, key, push):
        nonlocal count
        count += 1
        queue[link_of(push[0], push[4], push[5])].append(((kind, push[0], count), size, key, push))

    def spread(h, f):
        put(2, 1.0, (h, f, 3), (h, f, 0, None, 1, 1))
        put(2, 1.0, (h, f, 1), (h, f, 0, None, 1, -1))

    while len(order) < NQ * 40:
        arrivals.sort()
        if starts and starts[0][0] <= now:
            h = starts.pop(0)[1]
            order.append(("begin", h))
            now += 0.3
            put(0, 1.0, (h, 3, 0), (h, 0, 0, None, 0, 1))
            put(0, 1.0, (h, 1, 0), (h, 0, 0, None, 0, -1))
            spread(h, 0)
            both[h, 0, 0] = now + core_lat
            continue
        if arrivals and arrivals[0][0] <= now:
            h, f, s = arrivals.pop(0)[1]
            if f == 2 and s == 0 or s == 2:
                parts[h, f, s] = parts.get((h, f, s), 0) + 1
                if parts[h, f, s] < 2:
                    continue
            order.append(("forward", h, f, s))
            if s == 0:
                if f != 2:
                    step = 1 if f == 3 else -1
                    put(1, 0.5, (h, 2, 0), (h, f, 0, 0 if f == 3 else 1, 0, step))
                spread(h, f)
            elif s != 2:
                step = 1 if s == 3 else -1
                put(3, 0.5, (h, f, 2), (h, f, s, 0 if s == 3 else 1, 1, step))
            both[h, f, s] = now + core_lat
            now += 0.08
            continue
        sent = False
        for link in range(4):
            if queue[link] and (len(done[link]) < DEEP or done[link][-DEEP] <= now):
                queue[link].sort()
                _, size, key, push = queue[link].pop(0)
                free[link] = max(now, free[link]) + size * hop
                done[link].append(free[link])
                arrivals.append((free[link] + lat, key))
                order.append(("push",) + push)
                now += 0.04
                sent = True
                break
        if sent:
            continue
        ready = None
        for h, rel in todo:
            need = [(h, i, rel) if h % 2 == 0 else (h, rel, i) for i in range(4)]
            if all(both.get(k, 1e9) <= now for k in need):
                ready = (h, rel)
                break
        if ready:
            todo.remove(ready)
            order.append(("compute",) + ready)
            now += work
            continue
        times = [t for t, _ in arrivals[:1]] + [t for t, _ in starts[:1]]
        times += [t for t in both.values() if t > now]
        times += [
            done[link][-DEEP] for link in range(4)
            if queue[link] and len(done[link]) >= DEEP and done[link][-DEEP] > now
        ]
        now = max(now + 1e-3, min(times))
    return order


ORDER = plan()


def iota(shape, axis):
    return lax.broadcasted_iota(jnp.int32, shape, axis)


def div12(v):
    return (v * 5462) >> 16


def one_hot(cond):
    return jnp.where(cond, 1.0, 0.0).astype(BF16)


def dot(a, b, dims=((1,), (0,)), precision=None):
    return lax.dot_general(
        a, b, (dims, ((), ())), precision=precision, preferred_element_type=F32
    )


def eliminate(gram):
    row, lane = iota((RANK, 128), 0), iota((RANK, 128), 1)
    work = gram + jnp.where(lane == row + RANK, 1.0, 0.0)
    for k in range(RANK):
        column = jnp.broadcast_to(work[:, k:k + 1], (RANK, 128))
        scale = lax.rsqrt(column[k:k + 1, :])
        pivot_row = work[k:k + 1, :] * scale
        below = work - (column * scale) * pivot_row
        work = jnp.where(row > k, below, jnp.where(row == k, pivot_row, work))
    inverse = pltpu.roll(work, 128 - RANK, 1)
    return jnp.where(lane < RANK, inverse, 0.0)


def main_kernel(
    hid_hbm, og_hbm, q_hbm, res_hbm,
    mer_out, pb_out, qt_out, low_out,
    hid, og, pack, zbuf, grads, hid_t, res, mer, qv, pacc, pt_mine, pt_other, pg, pb, low,
    wb, wr, c2r, w2, c3r, gram_c, gram_p, gram_z, zw, qt,
    z_send, z_sem, link_send, xy_sem, core_send, core_sem, sends, b_sem, gc_sem, c1_sem,
    gp_sem, c2_sem, c3_sem, gz_sem, zw_sem, pz_sem, px_sem, pc_sem, ag_sem, agc_sem,
    local_sem, out_sem,
):
    dp, y = lax.axis_index("dp"), lax.axis_index("tensor")
    z, x, c = dp // 8, (dp // 2) % 4, dp % 2
    other = 1 - c
    replica = z // 4

    def device(dz=0, dx=0, dc=0, dy=0):
        return (((z + dz) % NZ) * 8 + ((x + dx) % NX) * 2 + (c + dc) % NC, (y + dy) % NY)

    sibling = device(dc=1)

    def remote(src, dst, send_sem, recv_sem, there):
        return pltpu.make_async_remote_copy(
            src_ref=src, dst_ref=dst, send_sem=send_sem, recv_sem=recv_sem,
            device_id=there, device_id_type=MESH,
        )

    def send(src, dst, send_sem, recv_sem, there):
        copy = remote(src, dst, send_sem, recv_sem, there)
        copy.start()
        return copy

    def arrived(ref, sem):
        remote(ref, ref, core_send.at[0], sem, sibling).wait_recv()

    def left(ref, sem):
        remote(ref, ref, sem, b_sem.at[0], sibling).wait_send()

    pending = []

    def later(ref, number):
        pending.append((ref, sends.at[number]))

    barrier = pltpu.get_barrier_semaphore()
    partners = [device(dz=d) for d in range(1, NZ)] + [sibling]
    partners += [
        device(dx=dx, dy=dy) for dx in range(NX) for dy in range(NY) if (dx, dy) != (0, 0)
    ]
    for partner in partners:
        pl.semaphore_signal(barrier, inc=1, device_id=partner, device_id_type=MESH)

    og_copy = pltpu.make_async_copy(og_hbm, og, local_sem.at[0])
    hid_copy = pltpu.make_async_copy(hid_hbm, hid, local_sem.at[1])
    q_copy = pltpu.make_async_copy(q_hbm, qv, local_sem.at[2])
    res_copy = pltpu.make_async_copy(res_hbm, res, local_sem.at[3])
    for copy in (og_copy, hid_copy, q_copy, res_copy):
        copy.start()

    og_copy.wait()
    total = jnp.zeros((48, 1024), F32)
    for g in range(4):
        pick = one_hot(iota((48, TOK_DEV), 0) == iota((48, TOK_DEV), 1) + g * TOK_DEV)
        lanes = [og[:, i * 512 + g * 128:i * 512 + (g + 1) * 128] for i in range(8)]
        total += dot(pick, jnp.concatenate(lanes, axis=1))
    for i in range(8):
        pack[i] = total[:, i * 128:(i + 1) * 128].astype(BF16)
    for h in range(NQ):
        zbuf[h * NZ + z] = pack[replica * NQ + h]

    pl.semaphore_wait(barrier, len(partners))

    def send_z(h):
        if h:
            left(zbuf.at[pl.ds(0, 7)], z_send.at[h - 1])
        for d in ALONG_Z:
            there = (z + d) % NZ // 4
            send(
                pack.at[there * NQ + h], zbuf.at[h * NZ + z], z_send.at[h], z_sem.at[h],
                device(dz=d),
            )

    send_z(0)

    hid_copy.wait()
    hidden = hid[...]
    for i in range(3):
        r = iota((1, 256), 1) + i * 256
        rx = jnp.where(r >= 192, 1, 0) + jnp.where(r >= 384, 1, 0) + jnp.where(r >= 576, 1, 0)
        r = r - rx * 192
        rc = jnp.where(r >= 96, 1, 0)
        r = r - rc * 96
        rz = div12(r)
        token = rz * 96 + rx * 24 + rc * 12 + (r - rz * 12)
        pick = one_hot(iota((TOK, 256), 0) == token)
        hid_t[:, i * 256:(i + 1) * 256] = dot(hidden, pick).astype(BF16)
    send_z(1)
    pacc[...] = jnp.zeros_like(pacc)
    pt_mine[...] = jnp.zeros_like(pt_mine)
    res_copy.wait()
    q_copy.wait()

    def block(h, first, second, part=None, core=None):
        dx, dy = (first, second) if h % 2 == 0 else (second, first)
        row = (x + dx) % NX * 192 + (c if core is None else core) * 96
        count = 96
        if part is not None:
            row, count = row + 48 * part, 48
        return grads.at[(y + dy) % NY * NQ + h, pl.ds(pl.multiple_of(row, 16), count)]

    flights = [[] for _ in range(4)]

    def push(h, first, second, part, axis, step):
        link = link_of(h, axis, step)
        number = len(flights[link])
        if number >= DEEP:
            flights[link][number - DEEP].wait_send()
        there = device(dx=step) if link < 2 else device(dy=step)
        f, s = first, second
        if axis == 0:
            f = (first - step) % 4
        else:
            s = (second - step) % 4
        ref = block(h, first, second, part)
        flights[link].append(
            send(ref, ref, link_send.at[link, number % DEEP], xy_sem.at[h, f * 4 + s], there)
        )

    def share(h, first, second):
        ref = block(h, first, second)
        rel = second if h % 2 == 0 else first
        send(ref, ref, core_send.at[0], core_sem.at[h, rel], sibling)

    def begin(h):
        if h + 2 < NQ:
            send_z(h + 2)
        arrived(zbuf.at[pl.ds(0, 7)], z_sem.at[h])
        packed = zbuf[h * NZ:(h + 1) * NZ].reshape(384, 128)
        row = pl.multiple_of(x * 192 + c * 96, 16)
        for g in range(4):
            r, s = iota((96, 384), 0), iota((96, 384), 1)
            pick = one_hot(s == r + div12(r) * 36 + g * TOK_DEV)
            grads[y * NQ + h, pl.ds(row, 96), g * 128:(g + 1) * 128] = dot(pick, packed).astype(BF16)
        share(h, 0, 0)

    def forward(h, f, s):
        arrived(block(h, f, s), xy_sem.at[h, f * 4 + s])
        share(h, f, s)

    blocks_out = []

    def add_left(cols):
        pacc[...] += dot(qv[:, cols], mer[:, cols], ((1,), (1,)))

    def compute(h, rel):
        arrived(grads.at[0, pl.ds(0, 384)], core_sem.at[h, rel])
        yb = (y + rel) % NY
        base = pl.multiple_of(yb * 2048 + h * 512, 512)

        def tile(i, carry):
            col = pl.multiple_of(base + i * 256, 256)
            part = grads[yb * NQ + h, :, pl.ds(pl.multiple_of(i * 256, 256), 256)]
            merged = dot(hid_t[...], part) + res[:, pl.ds(col, 256)].astype(F32)
            mer[:, pl.ds(col, 256)] = merged.astype(BF16)
            return carry

        if blocks_out:
            add_left(blocks_out[-1])
        lax.fori_loop(0, 2, tile, 0, unroll=True)
        cols = pl.ds(base, 512)
        pltpu.make_async_copy(mer.at[:, cols], mer_out.at[:, cols], out_sem.at[0]).start()
        blocks_out.append(cols)

    steps = {"begin": begin, "forward": forward, "compute": compute, "push": push}
    for what, *where in ORDER:
        steps[what](*where)

    def end():
        for ref, sem in pending:
            left(ref, sem)
        left(zbuf.at[pl.ds(0, 7)], z_send.at[NQ - 1])
        for link in range(4):
            for copy in flights[link][-DEEP:]:
                copy.wait_send()
        left(grads.at[pl.ds(0, 8)], core_send.at[0])
        pltpu.make_async_copy(mer, mer_out, out_sem.at[0]).wait()

    add_left(blocks_out[-1])
    pt_mine[:, 0:ROWS] = pacc[...]
    send(pt_mine, pt_other, sends.at[0], b_sem.at[0], device(dz=4))
    later(pt_mine, 0)
    arrived(pt_other, b_sem.at[0])
    pt = pt_mine[...] + pt_other[...]
    slot = c * 16 + z % 4 * 4 + x
    pg[slot] = pt

    gram = dot(pt, jnp.concatenate([pt, jnp.zeros((96, PAD), F32)], axis=0), ((1,), (1,)), HIGH)
    packed = gram[0:8]
    for g in range(1, 4):
        packed += pltpu.roll(gram[8 * g:8 * g + 8], 32 * g, 1)
    gram_c[0] = packed
    send(gram_c.at[0], gram_c.at[1], sends.at[1], gc_sem.at[0], sibling)
    later(gram_c.at[0], 1)

    hi = pt.astype(BF16)
    rest = pt - hi.astype(F32)
    mid = rest.astype(BF16)
    rest = (rest - mid.astype(F32)).astype(BF16)
    terms = jnp.concatenate([hi, mid, rest], axis=0)[:, :ROWS]

    def w_tiles(first):
        def tile(i, carry):
            nb = first + i * 2
            col = pl.multiple_of(nb * 128, 256)
            product = dot(terms, mer[:, pl.ds(col, 256)])
            total = product[0:32] + (product[32:64] + product[64:96])
            wb[nb] = total[:, 0:128]
            wb[nb + 1] = total[:, 128:256]
            return carry

        lax.fori_loop(0, 8, tile, 0, unroll=True)

    for h in range(2):
        w_tiles(other * 32 + h * 16)
        send(
            wb.at[pl.ds(other * 32 + h * 16, 16)], wr.at[pl.ds(h * 16, 16)],
            sends.at[2], c1_sem.at[h], sibling,
        )
        if h:
            continue
        for d in range(1, 4):
            send(pg.at[slot], pg.at[slot], sends.at[3], px_sem.at[0], device(dx=d))
        later(pg.at[pl.ds(0, 3)], 3)
        arrived(gram_c.at[0], gc_sem.at[0])
        spot = x * 4 + y
        gram_p[spot] = gram_c[0] + gram_c[1]
        for dx, dy in PLANE:
            send(
                gram_p.at[spot], gram_p.at[spot], sends.at[4], gp_sem.at[0],
                device(dx=dx, dy=dy),
            )
        later(gram_p.at[pl.ds(0, 15)], 4)
    later(wr, 2)
    places = (x, y)

    for h in range(2):
        w_tiles(c * 32 + h * 16)
        arrived(wr.at[pl.ds(h * 16, 16)], c1_sem.at[h])
        at = pl.ds(c * 32 + h * 16, 16)
        wb[at] = wb[at] + wr[pl.ds(h * 16, 16)]
        for d in (2, 1, 3):
            there = (places[h] + d) % 4
            send(
                wb.at[pl.ds(c * 32 + h * 16 + there * 4, 4)], c2r.at[h * 4 + places[h]],
                sends.at[5], c2_sem.at[h], device(dx=d) if h == 0 else device(dy=d),
            )
    later(c2r.at[pl.ds(0, 6)], 5)

    arrived(gram_p.at[pl.ds(0, 15)], gp_sem.at[0])
    total = gram_p[0]
    for i in range(1, 16):
        total += gram_p[i]
    gram_z[z] = total
    for d in ALONG_Z:
        send(gram_z.at[z], gram_z.at[z], sends.at[9], gz_sem.at[0], device(dz=d))
    later(gram_z.at[pl.ds(0, 7)], 9)

    arrived(pg.at[pl.ds(0, 3)], px_sem.at[0])
    group = pg.at[pl.ds(c * 16 + z % 4 * 4, 4)]
    for d in (1, -1, 2):
        send(group, group, sends.at[8], pz_sem.at[0], device(dz=d))
    later(pg.at[pl.ds(0, 12)], 8)

    for h in range(2):
        arrived(c2r.at[pl.ds(0, 3)], c2_sem.at[h])
        total = wb[pl.ds(c * 32 + h * 16 + places[h] * 4, 4)]
        for d in range(1, 4):
            total += c2r[h * 4 + (places[h] + d) % 4]
        w2[h] = total
        for d in (2, 1, 3):
            there = (places[1 - h] + d) % 4
            send(
                w2.at[h, there], c3r.at[h * 4 + places[1 - h]],
                sends.at[7], c3_sem.at[h], device(dy=d) if h == 0 else device(dx=d),
            )
    later(c3r.at[pl.ds(0, 6)], 7)

    arrived(gram_z.at[pl.ds(0, 7)], gz_sem.at[0])
    total = gram_z[0]
    for i in range(1, NZ):
        total += gram_z[i]
    total = total * 0.5
    lane = iota((RANK, 128), 1)
    gram = jnp.concatenate(
        [total] + [pltpu.roll(total, 128 - 32 * g, 1) for g in range(1, 4)], axis=0
    )
    inverse = eliminate(jnp.where(lane < RANK, gram, 0.0))[:, 0:RANK]

    for h in range(2):
        arrived(c3r.at[pl.ds(0, 3)], c3_sem.at[h])
        total = w2[h, places[1 - h]]
        for d in range(1, 4):
            total += c3r[h * 4 + (places[1 - h] + d) % 4]
        zw[h * NZ + z] = (dot(inverse, total, precision=HIGH) * 0.5).astype(BF16)
        for d in ALONG_Z:
            send(zw.at[h * NZ + z], zw.at[h * NZ + z], sends.at[10], zw_sem.at[h], device(dz=d))
    later(zw.at[pl.ds(0, 14)], 10)

    arrived(pg.at[pl.ds(0, 12)], pz_sem.at[0])
    half = pg.at[pl.ds(c * 16, 16)]
    send(half, half, sends.at[14], pc_sem.at[0], sibling)
    later(half, 14)
    own = dot(inverse, pg[slot], precision=HIGH)
    own = jnp.concatenate([own, jnp.zeros((96, PAD), F32)], axis=0).T
    low[...] = own[0:ROWS].astype(BF16)
    low_copy = pltpu.make_async_copy(low, low_out, local_sem.at[0])
    low_copy.start()

    mine = c * 16 + x * 4 + y
    for h in range(2):
        arrived(zw.at[pl.ds(0, 7)], zw_sem.at[h])
        total = zw[h * NZ].astype(F32)
        for i in range(1, NZ):
            total += zw[h * NZ + i].astype(F32)
        qt[h, mine] = total.astype(BF16)
        for dx, dy in PLANE:
            send(
                qt.at[h, mine], qt.at[h, mine], sends.at[11 + h],
                ag_sem.at[h * dx + h], device(dx=dx, dy=dy),
            )
        later(qt.at[h, pl.ds(0, 15)], 11 + h)

    arrived(half, pc_sem.at[0])
    for i in range(8):
        blocks = []
        for p in range(4 * i, 4 * i + 4):
            blocks.append(pg[p % 2 * 16 + p // 8 * 4 + p // 2 % 4][:, 0:ROWS])
        blocks = jnp.concatenate(blocks, axis=1)
        pb[:, i * 896:(i + 1) * 896] = dot(inverse, blocks, precision=HIGH)
    pb_copy = pltpu.make_async_copy(pb, pb_out, local_sem.at[1])
    pb_copy.start()

    arrived(qt.at[0, pl.ds(0, 15)], ag_sem.at[0])
    ours = qt.at[0, pl.ds(c * 16, 16)]
    send(ours, ours, sends.at[13], agc_sem.at[0], sibling)
    for dx in (0, 1, 3, 2):
        rows = qt.at[1, pl.ds(c * 16 + (x + 4 - dx) % 4 * 4, 4)]
        arrived(qt.at[1, pl.ds(0, 4 if dx else 3)], ag_sem.at[1 + dx])
        send(rows, rows, sends.at[13], agc_sem.at[0], sibling)
    later(qt.at[0], 13)
    arrived(qt.at[0], agc_sem.at[0])
    qt_copy = pltpu.make_async_copy(qt, qt_out, local_sem.at[2])
    qt_copy.start()
    end()
    low_copy.wait()
    pb_copy.wait()
    qt_copy.wait()


def exchange(
    hidden, out_grads, q_prev, residual,
):
    dma = pltpu.SemaphoreType.DMA
    any_spec = pl.BlockSpec(memory_space=pl.ANY)
    return pl.pallas_call(
        main_kernel,
        out_shape=(
            jax.ShapeDtypeStruct((ROWS, D), BF16),
            jax.ShapeDtypeStruct((RANK, 32 * ROWS), F32),
            jax.ShapeDtypeStruct((2, 32, RANK, 128), BF16),
            jax.ShapeDtypeStruct((ROWS, 128), BF16),
        ),
        in_specs=[any_spec] * 4,
        out_specs=(any_spec,) * 4,
        scratch_shapes=[
            pltpu.VMEM((ROWS, TOK), BF16),
            pltpu.VMEM((TOK_DEV, 4096), BF16),
            pltpu.VMEM((8, 48, 128), BF16),
            pltpu.VMEM((NQ * NZ, 48, 128), BF16),
            pltpu.VMEM((4 * NQ, TOK, 512), BF16),
            pltpu.VMEM((ROWS, TOK), BF16),
            pltpu.VMEM((ROWS, D), BF16),
            pltpu.VMEM((ROWS, D), BF16),
            pltpu.VMEM((RANK, D), BF16),
            pltpu.VMEM((RANK, ROWS), F32),
            pltpu.VMEM((RANK, PAD), F32),
            pltpu.VMEM((RANK, PAD), F32),
            pltpu.VMEM((32, RANK, PAD), F32),
            pltpu.VMEM((RANK, 32 * ROWS), F32),
            pltpu.VMEM((ROWS, 128), BF16),
            pltpu.VMEM((64, RANK, 128), F32),
            pltpu.VMEM((32, RANK, 128), F32),
            pltpu.VMEM((8, 4, RANK, 128), F32),
            pltpu.VMEM((2, 4, RANK, 128), F32),
            pltpu.VMEM((8, RANK, 128), F32),
            pltpu.VMEM((2, 8, 128), F32),
            pltpu.VMEM((16, 8, 128), F32),
            pltpu.VMEM((NZ, 8, 128), F32),
            pltpu.VMEM((2 * NZ, RANK, 128), BF16),
            pltpu.VMEM((2, 32, RANK, 128), BF16),
            dma((NQ,)),
            dma((NQ,)),
            dma((4, DEEP)),
            dma((NQ, 16)),
            dma((1,)),
            dma((NQ, 4)),
            dma((15,)),
            dma((1,)),
            dma((1,)),
            dma((2,)),
            dma((1,)),
            dma((2,)),
            dma((2,)),
            dma((1,)),
            dma((2,)),
            dma((1,)),
            dma((1,)),
            dma((1,)),
            dma((5,)),
            dma((1,)),
            dma((4,)),
            dma((1,)),
        ],
        name="exchange",
        compiler_params=pltpu.CompilerParams(
            collective_id=0, has_side_effects=True, vmem_limit_bytes=60 * 2**20
        ),
    )(hidden, out_grads, q_prev, residual)


def final_kernel(
    mer_hbm, pb_hbm, qt_hbm, low_hbm, res_hbm, p_hbm, q_hbm,
    mer, res, qt, low, q_new, pb, in_sem, out_sem,
):
    low_copy = pltpu.make_async_copy(low_hbm, low, in_sem.at[0])
    qt_copy = pltpu.make_async_copy(qt_hbm, qt, in_sem.at[1])
    p_copy = pltpu.make_async_copy(pb_hbm, pb, in_sem.at[2])
    low_copy.start()
    qt_copy.start()
    pieces = []
    for i in range(4):
        cols = pl.ds(i * 2048, 2048)
        pieces.append(pltpu.make_async_copy(mer_hbm.at[:, cols], mer.at[:, cols], in_sem.at[3 + i]))
        pieces[-1].start()
    p_copy.start()

    def place(nb):
        core, part, v = nb // 32, nb % 32 // 16, nb % 16
        return part, core * 16 + (v if part == 0 else v % 4 * 4 + v // 4)

    low_copy.wait()
    qt_copy.wait()
    p_low = low[:, 0:RANK]
    for i in range(4):
        pieces[i].wait()
        for nb in range(i * 16, i * 16 + 16, 2):
            q_low = jnp.concatenate([qt[place(nb)], qt[place(nb + 1)]], axis=1)
            cols = slice(nb * 128, nb * 128 + 256)
            res[:, cols] = (mer[:, cols].astype(F32) - dot(p_low, q_low)).astype(BF16)
        cols = pl.ds(i * 2048, 2048)
        pltpu.make_async_copy(res.at[:, cols], res_hbm.at[:, cols], out_sem.at[0]).start()
        if i == 0:
            p_copy.wait()
            p_copy = pltpu.make_async_copy(pb, p_hbm, in_sem.at[2])
            p_copy.start()

    nb = lax.axis_index("dp")
    part, v = nb % 32 // 16, nb % 16
    slot = nb // 32 * 16 + jnp.where(part == 0, v, v % 4 * 4 + v // 4)
    q_new[...] = qt[part, slot].astype(F32)
    q_copy = pltpu.make_async_copy(q_new, q_hbm, in_sem.at[0])
    q_copy.start()
    q_copy.wait()
    p_copy.wait()
    pltpu.make_async_copy(res, res_hbm, out_sem.at[0]).wait()


def finish(mer, pb, qt, low):
    any_spec = pl.BlockSpec(memory_space=pl.ANY)
    return pl.pallas_call(
        final_kernel,
        out_shape=(
            jax.ShapeDtypeStruct((ROWS, D), BF16),
            jax.ShapeDtypeStruct((RANK, 32 * ROWS), F32),
            jax.ShapeDtypeStruct((RANK, 128), F32),
        ),
        in_specs=[any_spec] * 4,
        out_specs=(any_spec,) * 3,
        scratch_shapes=[
            pltpu.VMEM((ROWS, D), BF16),
            pltpu.VMEM((ROWS, D), BF16),
            pltpu.VMEM((2, 32, RANK, 128), BF16),
            pltpu.VMEM((ROWS, 128), BF16),
            pltpu.VMEM((RANK, 128), F32),
            pltpu.VMEM((RANK, 32 * ROWS), F32),
            pltpu.SemaphoreType.DMA((7,)),
            pltpu.SemaphoreType.DMA((1,)),
        ],
        name="finish",
        compiler_params=pltpu.CompilerParams(vmem_limit_bytes=60 * 2**20),
    )(mer, pb, qt, low)


def on_device(hidden_acts, out_grads, residual_in, q_prev):
    parts = exchange(hidden_acts[0].T, out_grads, q_prev.T, residual_in[0])
    residual_out, p_basis, q_new = finish(*parts)
    return p_basis.T, q_new.T, residual_out[None]


def solution(mesh):
    in_specs = (P("dp", None, "tensor"), P("dp", "tensor"), P("dp", "tensor", None), P())
    out_specs = (P("tensor", None), P("dp", None), P("dp", "tensor", None))
    return jax.shard_map(
        on_device, mesh=mesh, in_specs=in_specs, out_specs=out_specs, check_vma=False
    )
```

```python
import jax
import jax.numpy as jnp
from jax import lax
from jax.experimental import pallas as pl
from jax.experimental.pallas import tpu as pltpu
from jax.sharding import PartitionSpec as P

NZ, NX, NC, NY = 8, 4, 2, 4
RANK = 32
TOK, TOK_DEV = 768, 12
ROWS = 224
D = 8192
PAD = 256
NQ = 4
DEEP = 2
PLANE = sorted(
    [(dx, dy) for dx in range(NX) for dy in range(NY) if (dx, dy) != (0, 0)],
    key=lambda o: -min(o[0], NX - o[0]) - min(o[1], NY - o[1]),
)
ALONG_Z = (4, 3, 5, 2, 6, 1, 7)
F32, BF16 = jnp.float32, jnp.bfloat16
HIGH = lax.Precision.HIGHEST
MESH = pl.DeviceIdType.MESH


def link_of(h, axis, step):
    return 2 * ((axis + h) % 2) + (0 if step == 1 else 1)


def plan():
    hop, lat, core_lat, work = 2.1, 2.8, 1.6, 0.65
    now, count, order, arrivals = 0.0, 0, [], []
    parts, both = {}, {}
    queue, done, free = [[] for _ in range(4)], [[] for _ in range(4)], [0.0] * 4
    starts = [(4.6 + 2.1 * h, h) for h in range(NQ)]
    todo = [(h, rel) for h in range(NQ) for rel in (0, 3, 1, 2)]

    def put(kind, size, key, push):
        nonlocal count
        count += 1
        queue[link_of(push[0], push[4], push[5])].append(((kind, push[0], count), size, key, push))

    def spread(h, f):
        put(2, 1.0, (h, f, 3), (h, f, 0, None, 1, 1))
        put(2, 1.0, (h, f, 1), (h, f, 0, None, 1, -1))

    while len(order) < NQ * 40:
        arrivals.sort()
        if starts and starts[0][0] <= now:
            h = starts.pop(0)[1]
            order.append(("begin", h))
            now += 0.3
            put(0, 1.0, (h, 3, 0), (h, 0, 0, None, 0, 1))
            put(0, 1.0, (h, 1, 0), (h, 0, 0, None, 0, -1))
            spread(h, 0)
            both[h, 0, 0] = now + core_lat
            continue
        if arrivals and arrivals[0][0] <= now:
            h, f, s = arrivals.pop(0)[1]
            if f == 2 and s == 0 or s == 2:
                parts[h, f, s] = parts.get((h, f, s), 0) + 1
                if parts[h, f, s] < 2:
                    continue
            order.append(("forward", h, f, s))
            if s == 0:
                if f != 2:
                    step = 1 if f == 3 else -1
                    put(1, 0.5, (h, 2, 0), (h, f, 0, 0 if f == 3 else 1, 0, step))
                spread(h, f)
            elif s != 2:
                step = 1 if s == 3 else -1
                put(3, 0.5, (h, f, 2), (h, f, s, 0 if s == 3 else 1, 1, step))
            both[h, f, s] = now + core_lat
            now += 0.08
            continue
        sent = False
        for link in range(4):
            if queue[link] and (len(done[link]) < DEEP or done[link][-DEEP] <= now):
                queue[link].sort()
                _, size, key, push = queue[link].pop(0)
                free[link] = max(now, free[link]) + size * hop
                done[link].append(free[link])
                arrivals.append((free[link] + lat, key))
                order.append(("push",) + push)
                now += 0.04
                sent = True
                break
        if sent:
            continue
        ready = None
        for h, rel in todo:
            need = [(h, i, rel) if h % 2 == 0 else (h, rel, i) for i in range(4)]
            if all(both.get(k, 1e9) <= now for k in need):
                ready = (h, rel)
                break
        if ready:
            todo.remove(ready)
            order.append(("compute",) + ready)
            now += work
            continue
        times = [t for t, _ in arrivals[:1]] + [t for t, _ in starts[:1]]
        times += [t for t in both.values() if t > now]
        times += [
            done[link][-DEEP] for link in range(4)
            if queue[link] and len(done[link]) >= DEEP and done[link][-DEEP] > now
        ]
        now = max(now + 1e-3, min(times))
    return order


ORDER = plan()


def iota(shape, axis):
    return lax.broadcasted_iota(jnp.int32, shape, axis)


def div12(v):
    return (v * 5462) >> 16


def one_hot(cond):
    return jnp.where(cond, 1.0, 0.0).astype(BF16)


def dot(a, b, dims=((1,), (0,)), precision=None):
    return lax.dot_general(
        a, b, (dims, ((), ())), precision=precision, preferred_element_type=F32
    )


def eliminate(gram):
    row, lane = iota((RANK, 128), 0), iota((RANK, 128), 1)
    work = gram + jnp.where(lane == row + RANK, 1.0, 0.0)
    for k in range(RANK):
        column = jnp.broadcast_to(work[:, k:k + 1], (RANK, 128))
        scale = lax.rsqrt(column[k:k + 1, :])
        pivot_row = work[k:k + 1, :] * scale
        below = work - (column * scale) * pivot_row
        work = jnp.where(row > k, below, jnp.where(row == k, pivot_row, work))
    inverse = pltpu.roll(work, 128 - RANK, 1)
    return jnp.where(lane < RANK, inverse, 0.0)


def main_kernel(
    hid_hbm, og_hbm, q_hbm, res_hbm,
    mer_out, pb_out, qt_out, low_out,
    hid, og, pack, picks, zbuf, grads, hid_t, res, mer, qv, pacc, pt_mine, pt_other, pg, pb, low,
    wb, wr, c2r, w2, c3r, gram_c, gram_p, gram_z, zw, qt,
    z_send, z_sem, link_send, xy_sem, core_send, core_sem, sends, b_sem, gc_sem, c1_sem,
    gp_sem, c2_sem, c3_sem, gz_sem, zw_sem, pz_sem, px_sem, pc_sem, ag_sem, agc_sem,
    local_sem, out_sem,
):
    dp, y = lax.axis_index("dp"), lax.axis_index("tensor")
    z, x, c = dp // 8, (dp // 2) % 4, dp % 2
    other = 1 - c
    replica = z // 4

    def device(dz=0, dx=0, dc=0, dy=0):
        return (((z + dz) % NZ) * 8 + ((x + dx) % NX) * 2 + (c + dc) % NC, (y + dy) % NY)

    sibling = device(dc=1)

    def remote(src, dst, send_sem, recv_sem, there):
        return pltpu.make_async_remote_copy(
            src_ref=src, dst_ref=dst, send_sem=send_sem, recv_sem=recv_sem,
            device_id=there, device_id_type=MESH,
        )

    def send(src, dst, send_sem, recv_sem, there):
        copy = remote(src, dst, send_sem, recv_sem, there)
        copy.start()
        return copy

    def arrived(ref, sem):
        remote(ref, ref, core_send.at[0], sem, sibling).wait_recv()

    def left(ref, sem):
        remote(ref, ref, sem, b_sem.at[0], sibling).wait_send()

    pending = []

    def later(ref, number):
        pending.append((ref, sends.at[number]))

    barrier = pltpu.get_barrier_semaphore()
    partners = [device(dz=d) for d in range(1, NZ)] + [sibling]
    partners += [
        device(dx=dx, dy=dy) for dx in range(NX) for dy in range(NY) if (dx, dy) != (0, 0)
    ]
    for partner in partners:
        pl.semaphore_signal(barrier, inc=1, device_id=partner, device_id_type=MESH)

    og_copy = pltpu.make_async_copy(og_hbm, og, local_sem.at[0])
    hid_copy = pltpu.make_async_copy(hid_hbm, hid, local_sem.at[1])
    q_copy = pltpu.make_async_copy(q_hbm, qv, local_sem.at[2])
    res_copy = pltpu.make_async_copy(res_hbm, res, local_sem.at[3])
    for copy in (og_copy, hid_copy, q_copy, res_copy):
        copy.start()

    og_copy.wait()
    total = jnp.zeros((48, 1024), F32)
    for g in range(4):
        pick = one_hot(iota((48, TOK_DEV), 0) == iota((48, TOK_DEV), 1) + g * TOK_DEV)
        lanes = [og[:, i * 512 + g * 128:i * 512 + (g + 1) * 128] for i in range(8)]
        total += dot(pick, jnp.concatenate(lanes, axis=1))
    for i in range(8):
        pack[i] = total[:, i * 128:(i + 1) * 128].astype(BF16)
    for h in range(NQ):
        zbuf[h * NZ + z] = pack[replica * NQ + h]

    pl.semaphore_wait(barrier, len(partners))

    def send_z(h):
        if h:
            left(zbuf.at[pl.ds(0, 7)], z_send.at[h - 1])
        for d in ALONG_Z:
            there = (z + d) % NZ // 4
            send(
                pack.at[there * NQ + h], zbuf.at[h * NZ + z], z_send.at[h], z_sem.at[h],
                device(dz=d),
            )

    send_z(0)

    hid_copy.wait()
    hidden = hid[...]
    for i in range(3):
        r = iota((1, 256), 1) + i * 256
        rx = jnp.where(r >= 192, 1, 0) + jnp.where(r >= 384, 1, 0) + jnp.where(r >= 576, 1, 0)
        r = r - rx * 192
        rc = jnp.where(r >= 96, 1, 0)
        r = r - rc * 96
        rz = div12(r)
        token = rz * 96 + rx * 24 + rc * 12 + (r - rz * 12)
        pick = one_hot(iota((TOK, 256), 0) == token)
        hid_t[:, i * 256:(i + 1) * 256] = dot(hidden, pick).astype(BF16)
    send_z(1)
    r = iota((384, 1), 0)
    g = jnp.where(r >= 96, 1, 0) + jnp.where(r >= 192, 1, 0) + jnp.where(r >= 288, 1, 0)
    r = r - g * 96
    picks[...] = one_hot(iota((384, 384), 1) == r + div12(r) * 36 + g * TOK_DEV)
    pacc[...] = jnp.zeros_like(pacc)
    pt_mine[...] = jnp.zeros_like(pt_mine)
    res_copy.wait()
    q_copy.wait()

    def block(h, first, second, part=None, core=None):
        dx, dy = (first, second) if h % 2 == 0 else (second, first)
        row = (x + dx) % NX * 192 + (c if core is None else core) * 96
        count = 96
        if part is not None:
            row, count = row + 48 * part, 48
        return grads.at[(y + dy) % NY * NQ + h, pl.ds(pl.multiple_of(row, 16), count)]

    flights = [[] for _ in range(4)]

    def push(h, first, second, part, axis, step):
        link = link_of(h, axis, step)
        number = len(flights[link])
        if number >= DEEP:
            flights[link][number - DEEP].wait_send()
        there = device(dx=step) if link < 2 else device(dy=step)
        f, s = first, second
        if axis == 0:
            f = (first - step) % 4
        else:
            s = (second - step) % 4
        ref = block(h, first, second, part)
        flights[link].append(
            send(ref, ref, link_send.at[link, number % DEEP], xy_sem.at[h, f * 4 + s], there)
        )

    def share(h, first, second):
        ref = block(h, first, second)
        rel = second if h % 2 == 0 else first
        send(ref, ref, core_send.at[0], core_sem.at[h, rel], sibling)

    def begin(h):
        if h + 2 < NQ:
            send_z(h + 2)
        arrived(zbuf.at[pl.ds(0, 7)], z_sem.at[h])
        tokens = dot(picks[...], zbuf[h * NZ:(h + 1) * NZ].reshape(384, 128)).astype(BF16)
        row = pl.multiple_of(x * 192 + c * 96, 16)
        for g in range(4):
            grads[y * NQ + h, pl.ds(row, 96), g * 128:(g + 1) * 128] = tokens[g * 96:(g + 1) * 96]
        share(h, 0, 0)

    def forward(h, f, s):
        arrived(block(h, f, s), xy_sem.at[h, f * 4 + s])
        share(h, f, s)

    blocks_out = []

    def add_left(cols):
        pacc[...] += dot(qv[:, cols], mer[:, cols], ((1,), (1,)))

    def compute(h, rel):
        arrived(grads.at[0, pl.ds(0, 384)], core_sem.at[h, rel])
        yb = (y + rel) % NY
        base = pl.multiple_of(yb * 2048 + h * 512, 512)

        def tile(i, carry):
            col = pl.multiple_of(base + i * 256, 256)
            part = grads[yb * NQ + h, :, pl.ds(pl.multiple_of(i * 256, 256), 256)]
            merged = dot(hid_t[...], part) + res[:, pl.ds(col, 256)].astype(F32)
            mer[:, pl.ds(col, 256)] = merged.astype(BF16)
            return carry

        if blocks_out:
            add_left(blocks_out[-1])
        lax.fori_loop(0, 2, tile, 0, unroll=True)
        cols = pl.ds(base, 512)
        pltpu.make_async_copy(mer.at[:, cols], mer_out.at[:, cols], out_sem.at[0]).start()
        blocks_out.append(cols)

    steps = {"begin": begin, "forward": forward, "compute": compute, "push": push}
    for what, *where in ORDER:
        steps[what](*where)

    def end():
        for ref, sem in pending:
            left(ref, sem)
        left(zbuf.at[pl.ds(0, 7)], z_send.at[NQ - 1])
        for link in range(4):
            for copy in flights[link][-DEEP:]:
                copy.wait_send()
        left(grads.at[pl.ds(0, 8)], core_send.at[0])
        pltpu.make_async_copy(mer, mer_out, out_sem.at[0]).wait()

    add_left(blocks_out[-1])
    pt_mine[:, 0:ROWS] = pacc[...]
    send(pt_mine, pt_other, sends.at[0], b_sem.at[0], device(dz=4))
    later(pt_mine, 0)
    arrived(pt_other, b_sem.at[0])
    pt = pt_mine[...] + pt_other[...]
    slot = c * 16 + z % 4 * 4 + x
    pg[slot] = pt

    gram = dot(pt, jnp.concatenate([pt, jnp.zeros((96, PAD), F32)], axis=0), ((1,), (1,)), HIGH)
    packed = gram[0:8]
    for g in range(1, 4):
        packed += pltpu.roll(gram[8 * g:8 * g + 8], 32 * g, 1)
    gram_c[0] = packed
    send(gram_c.at[0], gram_c.at[1], sends.at[1], gc_sem.at[0], sibling)
    later(gram_c.at[0], 1)

    hi = pt.astype(BF16)
    rest = pt - hi.astype(F32)
    mid = rest.astype(BF16)
    rest = (rest - mid.astype(F32)).astype(BF16)
    terms = jnp.concatenate([hi, mid, rest], axis=0)[:, :ROWS]

    def w_tiles(first):
        def tile(i, carry):
            nb = first + i * 2
            col = pl.multiple_of(nb * 128, 256)
            product = dot(terms, mer[:, pl.ds(col, 256)])
            total = product[0:32] + (product[32:64] + product[64:96])
            wb[nb] = total[:, 0:128]
            wb[nb + 1] = total[:, 128:256]
            return carry

        lax.fori_loop(0, 8, tile, 0, unroll=True)

    for h in range(2):
        w_tiles(other * 32 + h * 16)
        send(
            wb.at[pl.ds(other * 32 + h * 16, 16)], wr.at[pl.ds(h * 16, 16)],
            sends.at[2], c1_sem.at[h], sibling,
        )
        if h:
            continue
        for d in range(1, 4):
            send(pg.at[slot], pg.at[slot], sends.at[3], px_sem.at[0], device(dx=d))
        later(pg.at[pl.ds(0, 3)], 3)
        arrived(gram_c.at[0], gc_sem.at[0])
        spot = x * 4 + y
        gram_p[spot] = gram_c[0] + gram_c[1]
        for dx, dy in PLANE:
            send(
                gram_p.at[spot], gram_p.at[spot], sends.at[4], gp_sem.at[0],
                device(dx=dx, dy=dy),
            )
        later(gram_p.at[pl.ds(0, 15)], 4)
    later(wr, 2)
    places = (x, y)

    for h in range(2):
        w_tiles(c * 32 + h * 16)
        arrived(wr.at[pl.ds(h * 16, 16)], c1_sem.at[h])
        at = pl.ds(c * 32 + h * 16, 16)
        wb[at] = wb[at] + wr[pl.ds(h * 16, 16)]
        for d in (2, 1, 3):
            there = (places[h] + d) % 4
            send(
                wb.at[pl.ds(c * 32 + h * 16 + there * 4, 4)], c2r.at[h * 4 + places[h]],
                sends.at[5], c2_sem.at[h], device(dx=d) if h == 0 else device(dy=d),
            )
    later(c2r.at[pl.ds(0, 6)], 5)

    arrived(gram_p.at[pl.ds(0, 15)], gp_sem.at[0])
    total = gram_p[0]
    for i in range(1, 16):
        total += gram_p[i]
    gram_z[z] = total
    for d in ALONG_Z:
        send(gram_z.at[z], gram_z.at[z], sends.at[9], gz_sem.at[0], device(dz=d))
    later(gram_z.at[pl.ds(0, 7)], 9)

    arrived(pg.at[pl.ds(0, 3)], px_sem.at[0])
    group = pg.at[pl.ds(c * 16 + z % 4 * 4, 4)]
    for d in (1, -1, 2):
        send(group, group, sends.at[8], pz_sem.at[0], device(dz=d))
    later(pg.at[pl.ds(0, 12)], 8)

    for h in range(2):
        arrived(c2r.at[pl.ds(0, 3)], c2_sem.at[h])
        total = wb[pl.ds(c * 32 + h * 16 + places[h] * 4, 4)]
        for d in range(1, 4):
            total += c2r[h * 4 + (places[h] + d) % 4]
        w2[h] = total
        for d in (2, 1, 3):
            there = (places[1 - h] + d) % 4
            send(
                w2.at[h, there], c3r.at[h * 4 + places[1 - h]],
                sends.at[7], c3_sem.at[h], device(dy=d) if h == 0 else device(dx=d),
            )
    later(c3r.at[pl.ds(0, 6)], 7)

    arrived(gram_z.at[pl.ds(0, 7)], gz_sem.at[0])
    total = gram_z[0]
    for i in range(1, NZ):
        total += gram_z[i]
    total = total * 0.5
    lane = iota((RANK, 128), 1)
    gram = jnp.concatenate(
        [total] + [pltpu.roll(total, 128 - 32 * g, 1) for g in range(1, 4)], axis=0
    )
    inverse = eliminate(jnp.where(lane < RANK, gram, 0.0))[:, 0:RANK]

    for h in range(2):
        arrived(c3r.at[pl.ds(0, 3)], c3_sem.at[h])
        total = w2[h, places[1 - h]]
        for d in range(1, 4):
            total += c3r[h * 4 + (places[1 - h] + d) % 4]
        zw[h * NZ + z] = (dot(inverse, total, precision=HIGH) * 0.5).astype(BF16)
        for d in ALONG_Z:
            send(zw.at[h * NZ + z], zw.at[h * NZ + z], sends.at[10], zw_sem.at[h], device(dz=d))
    later(zw.at[pl.ds(0, 14)], 10)

    arrived(pg.at[pl.ds(0, 12)], pz_sem.at[0])
    half = pg.at[pl.ds(c * 16, 16)]
    send(half, half, sends.at[14], pc_sem.at[0], sibling)
    later(half, 14)
    own = dot(inverse, pg[slot], precision=HIGH)
    own = jnp.concatenate([own, jnp.zeros((96, PAD), F32)], axis=0).T
    low[...] = own[0:ROWS].astype(BF16)
    low_copy = pltpu.make_async_copy(low, low_out, local_sem.at[0])
    low_copy.start()

    mine = c * 16 + x * 4 + y
    for h in range(2):
        arrived(zw.at[pl.ds(0, 7)], zw_sem.at[h])
        total = zw[h * NZ].astype(F32)
        for i in range(1, NZ):
            total += zw[h * NZ + i].astype(F32)
        qt[h, mine] = total.astype(BF16)
        for dx, dy in PLANE:
            send(
                qt.at[h, mine], qt.at[h, mine], sends.at[11 + h],
                ag_sem.at[h * dx + h], device(dx=dx, dy=dy),
            )
        later(qt.at[h, pl.ds(0, 15)], 11 + h)

    arrived(half, pc_sem.at[0])
    for i in range(8):
        blocks = []
        for p in range(4 * i, 4 * i + 4):
            blocks.append(pg[p % 2 * 16 + p // 8 * 4 + p // 2 % 4][:, 0:ROWS])
        blocks = jnp.concatenate(blocks, axis=1)
        pb[:, i * 896:(i + 1) * 896] = dot(inverse, blocks, precision=HIGH)
    pb_copy = pltpu.make_async_copy(pb, pb_out, local_sem.at[1])
    pb_copy.start()

    arrived(qt.at[0, pl.ds(0, 15)], ag_sem.at[0])
    ours = qt.at[0, pl.ds(c * 16, 16)]
    send(ours, ours, sends.at[13], agc_sem.at[0], sibling)
    for dx in (0, 1, 3, 2):
        rows = qt.at[1, pl.ds(c * 16 + (x + 4 - dx) % 4 * 4, 4)]
        arrived(qt.at[1, pl.ds(0, 4 if dx else 3)], ag_sem.at[1 + dx])
        send(rows, rows, sends.at[13], agc_sem.at[1], sibling)
    later(qt.at[0], 13)
    qt_copies = []
    for h in range(2):
        arrived(qt.at[0, pl.ds(0, 16)], agc_sem.at[h])
        qt_copies.append(pltpu.make_async_copy(qt.at[h], qt_out.at[h], local_sem.at[2 + h]))
        qt_copies[h].start()
    end()
    low_copy.wait()
    pb_copy.wait()
    for copy in qt_copies:
        copy.wait()


def exchange(
    hidden, out_grads, q_prev, residual,
):
    dma = pltpu.SemaphoreType.DMA
    any_spec = pl.BlockSpec(memory_space=pl.ANY)
    return pl.pallas_call(
        main_kernel,
        out_shape=(
            jax.ShapeDtypeStruct((ROWS, D), BF16),
            jax.ShapeDtypeStruct((RANK, 32 * ROWS), F32),
            jax.ShapeDtypeStruct((2, 32, RANK, 128), BF16),
            jax.ShapeDtypeStruct((ROWS, 128), BF16),
        ),
        in_specs=[any_spec] * 4,
        out_specs=(any_spec,) * 4,
        scratch_shapes=[
            pltpu.VMEM((ROWS, TOK), BF16),
            pltpu.VMEM((TOK_DEV, 4096), BF16),
            pltpu.VMEM((8, 48, 128), BF16),
            pltpu.VMEM((384, 384), BF16),
            pltpu.VMEM((NQ * NZ, 48, 128), BF16),
            pltpu.VMEM((4 * NQ, TOK, 512), BF16),
            pltpu.VMEM((ROWS, TOK), BF16),
            pltpu.VMEM((ROWS, D), BF16),
            pltpu.VMEM((ROWS, D), BF16),
            pltpu.VMEM((RANK, D), BF16),
            pltpu.VMEM((RANK, ROWS), F32),
            pltpu.VMEM((RANK, PAD), F32),
            pltpu.VMEM((RANK, PAD), F32),
            pltpu.VMEM((32, RANK, PAD), F32),
            pltpu.VMEM((RANK, 32 * ROWS), F32),
            pltpu.VMEM((ROWS, 128), BF16),
            pltpu.VMEM((64, RANK, 128), F32),
            pltpu.VMEM((32, RANK, 128), F32),
            pltpu.VMEM((8, 4, RANK, 128), F32),
            pltpu.VMEM((2, 4, RANK, 128), F32),
            pltpu.VMEM((8, RANK, 128), F32),
            pltpu.VMEM((2, 8, 128), F32),
            pltpu.VMEM((16, 8, 128), F32),
            pltpu.VMEM((NZ, 8, 128), F32),
            pltpu.VMEM((2 * NZ, RANK, 128), BF16),
            pltpu.VMEM((2, 32, RANK, 128), BF16),
            dma((NQ,)),
            dma((NQ,)),
            dma((4, DEEP)),
            dma((NQ, 16)),
            dma((1,)),
            dma((NQ, 4)),
            dma((15,)),
            dma((1,)),
            dma((1,)),
            dma((2,)),
            dma((1,)),
            dma((2,)),
            dma((2,)),
            dma((1,)),
            dma((2,)),
            dma((1,)),
            dma((1,)),
            dma((1,)),
            dma((5,)),
            dma((2,)),
            dma((4,)),
            dma((1,)),
        ],
        name="exchange",
        compiler_params=pltpu.CompilerParams(
            collective_id=0, has_side_effects=True, vmem_limit_bytes=60 * 2**20
        ),
    )(hidden, out_grads, q_prev, residual)


def final_kernel(
    mer_hbm, pb_hbm, qt_hbm, low_hbm, res_hbm, p_hbm, q_hbm,
    mer, res, qt, low, q_new, pb, in_sem, out_sem,
):
    low_copy = pltpu.make_async_copy(low_hbm, low, in_sem.at[0])
    qt_copy = pltpu.make_async_copy(qt_hbm, qt, in_sem.at[1])
    p_copy = pltpu.make_async_copy(pb_hbm, pb, in_sem.at[2])
    low_copy.start()
    qt_copy.start()
    pieces = []
    for i in range(4):
        cols = pl.ds(i * 2048, 2048)
        pieces.append(pltpu.make_async_copy(mer_hbm.at[:, cols], mer.at[:, cols], in_sem.at[3 + i]))
        pieces[-1].start()
    p_copy.start()

    def place(nb):
        core, part, v = nb // 32, nb % 32 // 16, nb % 16
        return part, core * 16 + (v if part == 0 else v % 4 * 4 + v // 4)

    low_copy.wait()
    qt_copy.wait()
    p_low = low[:, 0:RANK]
    for i in range(4):
        pieces[i].wait()
        for nb in range(i * 16, i * 16 + 16, 2):
            q_low = jnp.concatenate([qt[place(nb)], qt[place(nb + 1)]], axis=1)
            cols = slice(nb * 128, nb * 128 + 256)
            res[:, cols] = (mer[:, cols].astype(F32) - dot(p_low, q_low)).astype(BF16)
        cols = pl.ds(i * 2048, 2048)
        pltpu.make_async_copy(res.at[:, cols], res_hbm.at[:, cols], out_sem.at[0]).start()
        if i == 0:
            p_copy.wait()
            p_copy = pltpu.make_async_copy(pb, p_hbm, in_sem.at[2])
            p_copy.start()

    nb = lax.axis_index("dp")
    part, v = nb % 32 // 16, nb % 16
    slot = nb // 32 * 16 + jnp.where(part == 0, v, v % 4 * 4 + v // 4)
    q_new[...] = qt[part, slot].astype(F32)
    q_copy = pltpu.make_async_copy(q_new, q_hbm, in_sem.at[0])
    q_copy.start()
    q_copy.wait()
    p_copy.wait()
    pltpu.make_async_copy(res, res_hbm, out_sem.at[0]).wait()


def finish(mer, pb, qt, low):
    any_spec = pl.BlockSpec(memory_space=pl.ANY)
    return pl.pallas_call(
        final_kernel,
        out_shape=(
            jax.ShapeDtypeStruct((ROWS, D), BF16),
            jax.ShapeDtypeStruct((RANK, 32 * ROWS), F32),
            jax.ShapeDtypeStruct((RANK, 128), F32),
        ),
        in_specs=[any_spec] * 4,
        out_specs=(any_spec,) * 3,
        scratch_shapes=[
            pltpu.VMEM((ROWS, D), BF16),
            pltpu.VMEM((ROWS, D), BF16),
            pltpu.VMEM((2, 32, RANK, 128), BF16),
            pltpu.VMEM((ROWS, 128), BF16),
            pltpu.VMEM((RANK, 128), F32),
            pltpu.VMEM((RANK, 32 * ROWS), F32),
            pltpu.SemaphoreType.DMA((7,)),
            pltpu.SemaphoreType.DMA((1,)),
        ],
        name="finish",
        compiler_params=pltpu.CompilerParams(vmem_limit_bytes=60 * 2**20),
    )(mer, pb, qt, low)


def on_device(hidden_acts, out_grads, residual_in, q_prev):
    parts = exchange(hidden_acts[0].T, out_grads, q_prev.T, residual_in[0])
    residual_out, p_basis, q_new = finish(*parts)
    return p_basis.T, q_new.T, residual_out[None]


def solution(mesh):
    in_specs = (P("dp", None, "tensor"), P("dp", "tensor"), P("dp", "tensor", None), P())
    out_specs = (P("tensor", None), P("dp", None), P("dp", "tensor", None))
    return jax.shard_map(
        on_device, mesh=mesh, in_specs=in_specs, out_specs=out_specs, check_vma=False
    )
```
